32 devices in a mesh: dp: 8 (over z, y), tensor: 4 (over x, core).
Axes of the slice: x: 2, y: 2, z: 4, core: 2. Of those that a mesh axis runs over, the one named last changes fastest.
Arguments:
- tokens: bfloat16 [1024, 4096], P(('dp', 'tensor')), may hold values from -6 to 6
- upstream_grad: bfloat16 [1024, 4096], P(('dp', 'tensor')), may hold values from -6 to 6
- w_gate: bfloat16 [4096, 3584], P(None, 'tensor'), may hold values from -0.09375 to 0.09375
- w_up: bfloat16 [4096, 3584], P(None, 'tensor'), may hold values from -0.09375 to 0.09375
- w_down: bfloat16 [3584, 4096], P('tensor'), may hold values from -0.09375 to 0.09375
Outputs:
- grad_tokens: bfloat16 [1024, 4096], P(('dp', 'tensor'))
- grad_down: float32 [3584, 4096], P('tensor', 'dp')
The draws below stay inside these ranges and needn't reach their ends.
All inputs are finite; a program needn't handle non-finite values.
Results may differ from the reference program's by a relative error of at most 0.03.
Values may be sent and summed in bfloat16 or wider, within the bound.
A program may use at most 128 MiB of HBM per device.

```python
import jax
import jax.numpy as jnp
from jax import lax

D = 4096
F_DEV = 896
FF = 3584
TOKENS = 1024
N_TENSOR = 4


def spiked(values, rng, source, target, shards_of, factor):
    owner, partner = [(jnp.arange(values.shape[position]) // (values.shape[position] // shards_of)).reshape([-1 if axis == position else 1 for axis in range(values.ndim)]) for position in (source, target)]
    chosen = jax.random.permutation(rng, shards_of)[partner]
    strong = (owner == chosen) | (owner == (partner + shards_of // 2) % shards_of)
    return jnp.where(strong, factor * values, values)


def shard_levels(rng, extent, pieces, low, high):
    def one(axis_at, shards_of):
        draws = jax.random.uniform(jax.random.fold_in(jax.random.fold_in(rng, 6), axis_at), (shards_of,), jnp.float32, low / len(pieces), high / len(pieces))
        return jnp.repeat(jnp.exp(draws), extent[axis_at] // shards_of).reshape((-1,) + (1,) * (len(extent) - axis_at - 1))

    level = one(*pieces[0])
    for cut in pieces[1:]:
        level = level * one(*cut)
    return level


def normal_values(own_key, shape, width, reach, pieces=(), kind=jnp.bfloat16):
    values = width * jax.random.normal(own_key, shape, jnp.float32)
    if pieces:
        values = values * shard_levels(own_key, shape, pieces, -0.22, 0.18)
    return jnp.clip(values, -reach, reach).astype(kind)


def noise_with(rng, dims, deviation, limit, split, heavy, kind=jnp.bfloat16):
    array = deviation * jax.random.normal(rng, dims, jnp.float32)
    if split:
        array = array * shard_levels(rng, dims, split, -0.22, 0.18)
    return jnp.clip(spiked(array, jax.random.fold_in(rng, 3), *heavy), -limit, limit).astype(kind)


def setup_inputs(seed: int = 0) -> dict:
    seeds = jax.random.split(jax.random.key(seed), 6)
    tokens = normal_values(seeds[0], (TOKENS, D), 1.0, 6.0, ((0, 32),))
    upstream_grad = noise_with(seeds[1], (TOKENS, D), 1.0, 6.0, ((0, 32),), (0, 1, 32, 2.75))
    w_gate = normal_values(seeds[2], (D, FF), D ** -0.5, 0.09375, ((1, 4),))
    w_up = normal_values(seeds[3], (D, FF), D ** -0.5, 0.09375, ((1, 4),))
    w_down = normal_values(seeds[4], (FF, D), FF ** -0.5, 0.09375, ((0, 4),))
    return dict(tokens=tokens, upstream_grad=upstream_grad, w_gate=w_gate, w_up=w_up, w_down=w_down)


def reference(tokens, upstream_grad, w_gate, w_up, w_down):
    gate_pre = jnp.dot(tokens, w_gate, preferred_element_type=jnp.float32)
    up_pre = jnp.dot(tokens, w_up, preferred_element_type=jnp.float32)
    sig_gate = jax.nn.sigmoid(gate_pre)
    act_gate = gate_pre * sig_gate
    hidden = (act_gate * up_pre).astype(jnp.bfloat16)
    grad_hidden = jnp.dot(upstream_grad, w_down.T, preferred_element_type=jnp.float32).astype(jnp.bfloat16)
    hidden_f = grad_hidden.astype(jnp.float32)
    grad_gate = (hidden_f * up_pre * sig_gate * (1.0 + gate_pre * (1.0 - sig_gate))).astype(jnp.bfloat16)
    grad_up = (hidden_f * act_gate).astype(jnp.bfloat16)

    def add_block(running, block_index):
        first = (block_index * F_DEV).astype(jnp.int32)
        gate_blk = lax.dynamic_slice_in_dim(grad_gate, first, F_DEV, 1)
        up_blk = lax.dynamic_slice_in_dim(grad_up, first, F_DEV, 1)
        wgate_blk = lax.dynamic_slice_in_dim(w_gate, first, F_DEV, 1)
        wup_blk = lax.dynamic_slice_in_dim(w_up, first, F_DEV, 1)
        term = jnp.dot(gate_blk, wgate_blk.T, preferred_element_type=jnp.float32)
        term = term + jnp.dot(up_blk, wup_blk.T, preferred_element_type=jnp.float32)
        rounded = lax.optimization_barrier(term.astype(jnp.bfloat16))
        return running + rounded.astype(jnp.float32), None

    start_sum = jnp.zeros((TOKENS, D), jnp.float32)
    total, unused = lax.scan(add_block, start_sum, jnp.arange(N_TENSOR, dtype=jnp.int32))
    grad_tokens = total.astype(jnp.bfloat16)
    factor = float(TOKENS) ** -0.5
    grad_down = jnp.dot(hidden.T, upstream_grad, preferred_element_type=jnp.float32) * factor
    return grad_tokens, grad_down
```

```python
import functools

import jax
import jax.numpy as jnp
from jax import lax
from jax.experimental import pallas as pl
from jax.experimental.pallas import tpu as pltpu
from jax.sharding import PartitionSpec as P


def contract_rows(left, right):
    return lax.dot_general(
        left, right, (((0,), (0,)), ((), ())), preferred_element_type=jnp.float32
    )


def contract_cols(left, right):
    return lax.dot_general(
        left, right, (((1,), (1,)), ((), ())), preferred_element_type=jnp.float32
    )


def plain_body(tokens, upstream_grad, w_gate, w_up, w_down):
    n_dp = lax.axis_size("dp")
    rows, width = upstream_grad.shape
    gathered = lax.all_gather(tokens, "tensor", axis=0, tiled=True)
    upstream = lax.all_gather(upstream_grad, "tensor", axis=0, tiled=True)
    mine = lax.all_to_all(
        upstream_grad.reshape(rows, n_dp, width // n_dp), "dp", split_axis=1, concat_axis=0
    )
    mine = lax.all_gather(mine.reshape(n_dp, rows, width // n_dp), "tensor", axis=1, tiled=True)
    mine = mine.reshape(-1, width // n_dp)
    gate_pre = jnp.dot(gathered, w_gate, preferred_element_type=jnp.float32)
    up_pre = jnp.dot(gathered, w_up, preferred_element_type=jnp.float32)
    sig_gate = jax.nn.sigmoid(gate_pre)
    act_gate = gate_pre * sig_gate
    hidden = (act_gate * up_pre).astype(jnp.bfloat16)
    hidden_all = lax.all_gather(hidden, "dp", axis=0, tiled=True)
    grad_hidden = contract_cols(upstream, w_down).astype(jnp.bfloat16)
    hidden_f = grad_hidden.astype(jnp.float32)
    grad_gate = (hidden_f * up_pre * sig_gate * (1.0 + gate_pre * (1.0 - sig_gate))).astype(
        jnp.bfloat16
    )
    grad_up = (hidden_f * act_gate).astype(jnp.bfloat16)
    factor = float(hidden_all.shape[0]) ** (-0.5)
    summed = lax.psum_scatter(
        (contract_cols(grad_gate, w_gate) + contract_cols(grad_up, w_up)).astype(jnp.bfloat16),
        "tensor",
        scatter_dimension=0,
        tiled=True,
    )
    grad_down = contract_rows(hidden_all, mine) * factor
    return (summed, grad_down)


MESH = pl.DeviceIdType.MESH
BF16 = jnp.bfloat16
F32 = jnp.float32
PARTS = 4
UNITS = 256


def kernel(
    n_dp, n_tensor,
    tok, upg, wg_h, wu_h, wd_h,
    gtok_h, gdown_h,
    wg, wu, wd, gt, gu, gate, up, gh, gboth, hid, upc, part, pc_out, pc_in, cs_out, cs_in,
    gtok, gdown,
    w_sem, loc_sem, out_sem,
    core_s, core_r, x_s, x_r, fwd_s, fwd_r,
    a2a_s, a2a_r, uc_s, uc_r, ux_s, ux_r, uf_s, uf_r,
    hy_s, hy_r, hz_s, hz_r, hf_s, hf_r,
    pc_s, pc_r, cs_s, cs_r,
):
    rows, width = tok.shape
    units = wg_h.shape[1]
    replica = rows * n_tensor
    step = width // PARTS
    mine = width // n_dp
    n_x, n_z = n_tensor // 2, n_dp // 2
    d, t = lax.axis_index("dp"), lax.axis_index("tensor")
    c, x = lax.rem(t, 2), lax.div(t, 2)
    y, z = lax.rem(d, 2), lax.div(d, 2)
    core = (d, x * 2 + 1 - c)
    ypeer = (z * 2 + 1 - y, t)
    xs, zs = range(1, n_x), range(1, n_z)
    pieces = [(f, min(UNITS, units - f)) for f in range(0, units, UNITS)]

    def x_to(o):
        return (d, lax.rem(x + o, n_x) * 2 + c)

    def x_from(o):
        return lax.rem(x + n_x - o, n_x) * 2 + c

    def z_to(o):
        return (lax.rem(z + o, n_z) * 2 + y, t)

    def z_from(o):
        return lax.rem(z + n_z - o, n_z) * 2 + y

    def dp_to(o):
        return lax.rem(d + o, n_dp)

    def of_tensor(i):
        return pl.ds(pl.multiple_of(i * rows, rows), rows)

    def of_dp(i):
        return pl.ds(pl.multiple_of(i * replica, replica), replica)

    def cut(k):
        return pl.ds(k * step, step)

    def remote(src, dst, s, r, to):
        return pltpu.make_async_remote_copy(
            src_ref=src, dst_ref=dst, send_sem=s, recv_sem=r, device_id=to, device_id_type=MESH
        )

    loads = [[
        pltpu.make_async_copy(wg_h.at[cut(k), :], wg.at[cut(k), :], w_sem.at[0, k]),
        pltpu.make_async_copy(wu_h.at[cut(k), :], wu.at[cut(k), :], w_sem.at[1, k]),
        pltpu.make_async_copy(wd_h.at[:, cut(k)], wd.at[:, cut(k)], w_sem.at[2, k]),
    ] for k in range(PARTS)]
    own = [
        pltpu.make_async_copy(tok, gt.at[of_tensor(t), :], loc_sem.at[0]),
        pltpu.make_async_copy(upg, gu.at[of_tensor(t), :], loc_sem.at[1]),
        pltpu.make_async_copy(
            upg.at[:, pl.ds(pl.multiple_of(d * mine, mine), mine)],
            upc.at[d, of_tensor(t), :], loc_sem.at[2]),
    ]
    for copy in own:
        copy.start()
    for k in range(PARTS):
        loads[k][0].start()
        loads[k][1].start()

    barrier = pltpu.get_barrier_semaphore()
    pl.semaphore_signal(barrier, inc=1, device_id=core, device_id_type=MESH)
    for o in xs:
        pl.semaphore_signal(barrier, inc=1, device_id=x_to(o), device_id_type=MESH)
    for o in range(1, n_dp):
        pl.semaphore_signal(barrier, inc=1, device_id=(dp_to(o), t), device_id_type=MESH)
    pl.semaphore_wait(barrier, 1 + (n_x - 1) + (n_dp - 1))

    to_core, to_x, passed = {}, {}, {}
    for a, (src, dst) in enumerate(((tok, gt), (upg, gu))):
        for k in range(PARTS):
            to_core[a, k] = remote(
                src.at[:, cut(k)], dst.at[of_tensor(t), cut(k)],
                core_s.at[a, k], core_r.at[a, k], core)
            for o in xs:
                to_x[a, k, o] = remote(
                    src.at[:, cut(k)], dst.at[of_tensor(t), cut(k)],
                    x_s.at[a, k, o - 1], x_r.at[a, k, o - 1], x_to(o))
                there = dst.at[of_tensor(x_from(o)), cut(k)]
                passed[a, k, o] = remote(
                    there, there, fwd_s.at[a, k, o - 1], fwd_r.at[a, k, o - 1], core)
    for k in range(PARTS):
        for o in xs:
            to_x[0, k, o].start()
        to_core[0, k].start()
    exchange = [
        remote(
            upg.at[:, pl.ds(pl.multiple_of(dp_to(o) * mine, mine), mine)],
            upc.at[d, of_tensor(t), :],
            a2a_s.at[o - 1], a2a_r.at[o - 1], (dp_to(o), t))
        for o in range(1, n_dp)
    ]
    for copy in exchange:
        copy.start()
    for k in range(PARTS):
        to_core[1, k].start()

    def arrive(a, k):
        for o in xs:
            to_x[a, k, o].wait_recv()
            passed[a, k, o].start()

    def complete(a, k):
        to_core[a, k].wait_recv()
        for o in xs:
            passed[a, k, o].wait_recv()

    hid_y, hid_z, hid_f = {}, {}, {}
    for j, (f, n) in enumerate(pieces):
        here = hid.at[pl.ds(f, n), of_dp(d)]
        hid_y[j] = remote(here, here, hy_s.at[j], hy_r.at[j], ypeer)
        for o in zs:
            hid_z[j, o] = remote(here, here, hz_s.at[j, o - 1], hz_r.at[j, o - 1], z_to(o))
            there = hid.at[pl.ds(f, n), of_dp(z_from(o))]
            hid_f[j, o] = remote(there, there, hf_s.at[j, o - 1], hf_r.at[j, o - 1], ypeer)

    def pass_hidden(j):
        for o in zs:
            hid_z[j, o].wait_recv()
            hid_f[j, o].start()

    own[0].wait()
    for k in range(PARTS):
        arrive(0, k)
        for o in xs:
            to_x[1, k, o].start()
        loads[k][2].start()
        complete(0, k)
        loads[k][0].wait()
        loads[k][1].wait()
        lhs = gt[:, k * step:(k + 1) * step]
        for j, (f, n) in enumerate(pieces):
            fs, ks = slice(f, f + n), slice(k * step, (k + 1) * step)
            g = jnp.dot(lhs, wg[ks, fs], preferred_element_type=F32)
            u = jnp.dot(lhs, wu[ks, fs], preferred_element_type=F32)
            if k > 0:
                g, u = gate[:, fs] + g, up[:, fs] + u
            gate[:, fs] = g
            up[:, fs] = u
            if k == PARTS - 1:
                h = g * jax.nn.sigmoid(g) * u
                hid[fs, of_dp(d)] = h.T.astype(BF16)
                for o in zs:
                    hid_z[j, o].start()
                hid_y[j].start()

    own[2].wait()
    for copy in exchange:
        copy.wait_recv()
    block = upc.at[:, of_tensor(t), :]
    up_core = remote(block, block, uc_s, uc_r, core)
    up_core.start()
    up_x, up_f = {}, {}
    for o in xs:
        up_x[o] = remote(block, block, ux_s.at[o - 1], ux_r.at[o - 1], x_to(o))
        there = upc.at[:, of_tensor(x_from(o)), :]
        up_f[o] = remote(there, there, uf_s.at[o - 1], uf_r.at[o - 1], core)

    own[1].wait()
    for k in range(PARTS):
        arrive(1, k)
        complete(1, k)
        loads[k][2].wait()
        ks = slice(k * step, (k + 1) * step)
        lhs = gu[:, ks]
        for f, n in pieces:
            fs = slice(f, f + n)
            p = contract_cols(lhs, wd[fs, ks])
            if k > 0:
                p = gh[:, fs] + p
            gh[:, fs] = p
    for o in xs:
        up_x[o].start()
    for f, n in pieces:
        fs = slice(f, f + n)
        g, u = gate[:, fs], up[:, fs]
        h = gh[:, fs].astype(BF16).astype(F32)
        sig = jax.nn.sigmoid(g)
        gboth[:, fs] = (h * u * sig * (1.0 + g * (1.0 - sig))).astype(BF16)
        gboth[:, units + f:units + f + n] = (h * (g * sig)).astype(BF16)
    pass_hidden(0)

    swap, chip = {}, {}
    for q in range(PARTS):
        swap[q] = remote(
            pc_out.at[:, :, cut(q)], pc_in.at[:, :, cut(q)], pc_s.at[q], pc_r.at[q], core)
        for o in xs:
            chip[q, o] = remote(
                cs_out.at[o - 1, :, cut(q)], cs_in.at[o - 1, :, cut(q)],
                cs_s.at[q, o - 1], cs_r.at[q, o - 1], x_to(o))

    def add_cores(q):
        swap[q].wait_recv()
        qs = slice(q * step, (q + 1) * step)
        for o in xs:
            to = lax.rem(x + o, n_x)
            both = part[of_tensor(to * 2 + c), qs] + pc_in[to, :, qs].astype(F32)
            cs_out[o - 1, :, qs] = both.astype(BF16)
            chip[q, o].start()

    for q in range(PARTS):
        qs = slice(q * step, (q + 1) * step)
        part[:, qs] = contract_cols(gboth[:, :units], wg[qs, :]) + contract_cols(
            gboth[:, units:], wu[qs, :])
        for i in range(n_x):
            pc_out[i, :, qs] = part[of_tensor(i * 2 + 1 - c), qs].astype(BF16)
        swap[q].start()
        if q > 0:
            add_cores(q - 1)
    add_cores(PARTS - 1)
    pass_hidden(1)
    for o in xs:
        up_x[o].wait_recv()
        up_f[o].start()
    for q in range(PARTS):
        qs = slice(q * step, (q + 1) * step)
        total = part[of_tensor(t), qs] + pc_in[x, :, qs].astype(F32)
        for o in xs:
            chip[q, o].wait_recv()
            total = total + cs_in[o - 1, :, qs].astype(F32)
        gtok[:, qs] = total.astype(BF16)
    results = [pltpu.make_async_copy(gtok, gtok_h, out_sem.at[len(pieces)])]
    results[0].start()

    up_core.wait_recv()
    for o in xs:
        up_f[o].wait_recv()
    factor = float(n_dp * replica) ** (-0.5)
    for j, (f, n) in enumerate(pieces):
        if j + 2 < len(pieces):
            pass_hidden(j + 2)
        hid_y[j].wait_recv()
        for o in zs:
            hid_f[j, o].wait_recv()
        fs = slice(f, f + n)
        gdown[fs, :] = jnp.dot(
            hid[fs, :], upc[...].reshape(n_dp * replica, mine), preferred_element_type=F32
        ) * factor
        copy = pltpu.make_async_copy(
            gdown.at[pl.ds(f, n), :], gdown_h.at[pl.ds(f, n), :], out_sem.at[j])
        copy.start()
        results.append(copy)

    sent = [*to_core.values(), *to_x.values(), *passed.values(), *exchange, up_core,
            *up_x.values(), *up_f.values(), *hid_y.values(), *hid_z.values(), *hid_f.values(),
            *swap.values(), *chip.values()]
    for copy in sent:
        copy.wait_send()
    for copy in results:
        copy.wait()


def body(tokens, upstream_grad, w_gate, w_up, w_down):
    n_dp, n_tensor = lax.axis_size("dp"), lax.axis_size("tensor")
    rows, width = tokens.shape
    units = w_gate.shape[1]
    mine = width // n_dp
    n_x, n_z = n_tensor // 2, n_dp // 2
    if rows % 16 or n_tensor % 2 or n_dp % 2 or n_x < 2 or n_z < 2:
        return plain_body(tokens, upstream_grad, w_gate, w_up, w_down)
    replica = rows * n_tensor
    n_pieces = -(-units // UNITS)
    dma = pltpu.SemaphoreType.DMA
    vmem = pltpu.VMEM

    def pair(*shape):
        return [dma(shape), dma(shape)] if shape else [dma, dma]

    scratch = [
        vmem((width, units), BF16), vmem((width, units), BF16), vmem((units, width), BF16),
        vmem((replica, width), BF16), vmem((replica, width), BF16),
        vmem((replica, units), F32), vmem((replica, units), F32), vmem((replica, units), F32),
        vmem((replica, 2 * units), BF16),
        vmem((units, n_dp * replica), BF16),
        vmem((n_dp, replica, mine), BF16),
        vmem((replica, width), F32),
        vmem((n_x, rows, width), BF16), vmem((n_x, rows, width), BF16),
        vmem((n_x - 1, rows, width), BF16), vmem((n_x - 1, rows, width), BF16),
        vmem((rows, width), BF16), vmem((units, mine), F32),
        dma((3, PARTS)), dma((3,)), dma((n_pieces + 1,)),
        *pair(2, PARTS), *pair(2, PARTS, n_x - 1), *pair(2, PARTS, n_x - 1),
        *pair(n_dp - 1), *pair(), *pair(n_x - 1), *pair(n_x - 1),
        *pair(n_pieces), *pair(n_pieces, n_z - 1), *pair(n_pieces, n_z - 1),
        *pair(PARTS), *pair(PARTS, n_x - 1),
    ]
    return pl.pallas_call(
        functools.partial(kernel, n_dp, n_tensor),
        out_shape=(
            jax.ShapeDtypeStruct((rows, width), BF16),
            jax.ShapeDtypeStruct((units, mine), F32),
        ),
        in_specs=[pl.BlockSpec(memory_space=pl.ANY)] * 5,
        out_specs=(pl.BlockSpec(memory_space=pl.ANY),) * 2,
        scratch_shapes=scratch,
        compiler_params=pltpu.CompilerParams(
            collective_id=0, has_side_effects=True, vmem_limit_bytes=56 * 1024 * 1024
        ),
        cost_estimate=pl.CostEstimate(
            flops=2 * replica * width * units * 6, bytes_accessed=6 * width * units,
            transcendentals=replica * units,
        ),
    )(tokens, upstream_grad, w_gate, w_up, w_down)


def solution(mesh):
    in_specs = (
        P(("dp", "tensor"), None),
        P(("dp", "tensor"), None),
        P(None, "tensor"),
        P(None, "tensor"),
        P("tensor", None),
    )
    out_specs = (P(("dp", "tensor"), None), P("tensor", "dp"))
    return jax.shard_map(body, mesh=mesh, in_specs=in_specs, out_specs=out_specs, check_vma=False)
```

```python
import functools

import jax
import jax.numpy as jnp
from jax import lax
from jax.experimental import pallas as pl
from jax.experimental.pallas import tpu as pltpu
from jax.sharding import PartitionSpec as P


def contract_rows(left, right):
    return lax.dot_general(
        left, right, (((0,), (0,)), ((), ())), preferred_element_type=jnp.float32
    )


def contract_cols(left, right):
    return lax.dot_general(
        left, right, (((1,), (1,)), ((), ())), preferred_element_type=jnp.float32
    )


def plain_body(tokens, upstream_grad, w_gate, w_up, w_down):
    n_dp = lax.axis_size("dp")
    rows, width = upstream_grad.shape
    gathered = lax.all_gather(tokens, "tensor", axis=0, tiled=True)
    upstream = lax.all_gather(upstream_grad, "tensor", axis=0, tiled=True)
    mine = lax.all_to_all(
        upstream_grad.reshape(rows, n_dp, width // n_dp), "dp", split_axis=1, concat_axis=0
    )
    mine = lax.all_gather(mine.reshape(n_dp, rows, width // n_dp), "tensor", axis=1, tiled=True)
    mine = mine.reshape(-1, width // n_dp)
    gate_pre = jnp.dot(gathered, w_gate, preferred_element_type=jnp.float32)
    up_pre = jnp.dot(gathered, w_up, preferred_element_type=jnp.float32)
    sig_gate = jax.nn.sigmoid(gate_pre)
    act_gate = gate_pre * sig_gate
    hidden = (act_gate * up_pre).astype(jnp.bfloat16)
    hidden_all = lax.all_gather(hidden, "dp", axis=0, tiled=True)
    grad_hidden = contract_cols(upstream, w_down).astype(jnp.bfloat16)
    hidden_f = grad_hidden.astype(jnp.float32)
    grad_gate = (hidden_f * up_pre * sig_gate * (1.0 + gate_pre * (1.0 - sig_gate))).astype(
        jnp.bfloat16
    )
    grad_up = (hidden_f * act_gate).astype(jnp.bfloat16)
    factor = float(hidden_all.shape[0]) ** (-0.5)
    summed = lax.psum_scatter(
        (contract_cols(grad_gate, w_gate) + contract_cols(grad_up, w_up)).astype(jnp.bfloat16),
        "tensor",
        scatter_dimension=0,
        tiled=True,
    )
    grad_down = contract_rows(hidden_all, mine) * factor
    return (summed, grad_down)


MESH = pl.DeviceIdType.MESH
BF16 = jnp.bfloat16
F32 = jnp.float32
PARTS = 4
UNITS = 256


def kernel(
    n_dp, n_tensor,
    tok, upg, wg_h, wu_h, wd_h,
    gtok_h, gdown_h,
    wg, wu, wd, gt, gu, gate, up, gh, gboth, hid, upc, part, pc_out, pc_in, cs_out, cs_in,
    gtok, gdown,
    w_sem, loc_sem, out_sem,
    core_s, core_r, x_s, x_r, fwd_s, fwd_r,
    a2a_s, a2a_r, uc_s, uc_r, ux_s, ux_r, uf_s, uf_r,
    hy_s, hy_r, hz_s, hz_r, hf_s, hf_r,
    pc_s, pc_r, cs_s, cs_r,
):
    rows, width = tok.shape
    units = wg_h.shape[1]
    replica = rows * n_tensor
    step = width // PARTS
    mine = width // n_dp
    n_x, n_z = n_tensor // 2, n_dp // 2
    d, t = lax.axis_index("dp"), lax.axis_index("tensor")
    c, x = lax.rem(t, 2), lax.div(t, 2)
    y, z = lax.rem(d, 2), lax.div(d, 2)
    core = (d, x * 2 + 1 - c)
    ypeer = (z * 2 + 1 - y, t)
    xs, zs = range(1, n_x), range(1, n_z)
    pieces = [(f, min(UNITS, units - f)) for f in range(0, units, UNITS)]

    def x_to(o):
        return (d, lax.rem(x + o, n_x) * 2 + c)

    def x_from(o):
        return lax.rem(x + n_x - o, n_x) * 2 + c

    def z_to(o):
        return (lax.rem(z + o, n_z) * 2 + y, t)

    def z_from(o):
        return lax.rem(z + n_z - o, n_z) * 2 + y

    def dp_to(o):
        return lax.rem(d + o, n_dp)

    def of_tensor(i):
        return pl.ds(pl.multiple_of(i * rows, rows), rows)

    def of_chip(o):
        return pl.ds(pl.multiple_of(lax.rem(x + n_x - o, n_x) * 2 * rows, 2 * rows), 2 * rows)

    def cut(k):
        return pl.ds(k * step, step)

    def remote(src, dst, s, r, to):
        return pltpu.make_async_remote_copy(
            src_ref=src, dst_ref=dst, send_sem=s, recv_sem=r, device_id=to, device_id_type=MESH
        )

    loads = [[
        pltpu.make_async_copy(wg_h.at[cut(k), :], wg.at[cut(k), :], w_sem.at[0, k]),
        pltpu.make_async_copy(wu_h.at[cut(k), :], wu.at[cut(k), :], w_sem.at[1, k]),
        pltpu.make_async_copy(wd_h.at[:, cut(k)], wd.at[:, cut(k)], w_sem.at[2, k]),
    ] for k in range(PARTS)]
    own = [
        pltpu.make_async_copy(tok, gt.at[of_tensor(t), :], loc_sem.at[0]),
        pltpu.make_async_copy(upg, gu.at[of_tensor(t), :], loc_sem.at[1]),
        pltpu.make_async_copy(
            upg.at[:, pl.ds(pl.multiple_of(d * mine, mine), mine)],
            upc.at[d, of_tensor(t), :], loc_sem.at[2]),
    ]
    for copy in own:
        copy.start()
    for k in range(2):
        loads[k][0].start()
        loads[k][1].start()

    barrier = pltpu.get_barrier_semaphore()
    pl.semaphore_signal(barrier, inc=1, device_id=core, device_id_type=MESH)
    for o in xs:
        pl.semaphore_signal(barrier, inc=1, device_id=x_to(o), device_id_type=MESH)
    for o in range(1, n_dp):
        pl.semaphore_signal(barrier, inc=1, device_id=(dp_to(o), t), device_id_type=MESH)
    pl.semaphore_wait(barrier, 1 + (n_x - 1) + (n_dp - 1))

    to_core, to_x, passed = {}, {}, {}
    for a, (src, dst) in enumerate(((tok, gt), (upg, gu))):
        for k in range(PARTS):
            to_core[a, k] = remote(
                src.at[:, cut(k)], dst.at[of_tensor(t), cut(k)],
                core_s.at[a, k], core_r.at[a, k], core)
            for o in xs:
                to_x[a, k, o] = remote(
                    src.at[:, cut(k)], dst.at[of_tensor(t), cut(k)],
                    x_s.at[a, k, o - 1], x_r.at[a, k, o - 1], x_to(o))
                there = dst.at[of_tensor(x_from(o)), cut(k)]
                passed[a, k, o] = remote(
                    there, there, fwd_s.at[a, k, o - 1], fwd_r.at[a, k, o - 1], core)
    for k in range(PARTS):
        for o in xs:
            to_x[0, k, o].start()
        to_core[0, k].start()
    exchange = [
        remote(
            upg.at[:, pl.ds(pl.multiple_of(dp_to(o) * mine, mine), mine)],
            upc.at[d, of_tensor(t), :],
            a2a_s.at[o - 1], a2a_r.at[o - 1], (dp_to(o), t))
        for o in range(1, n_dp)
    ]
    for copy in exchange:
        copy.start()
    for k in range(PARTS):
        to_core[1, k].start()

    def arrive(a, k):
        for o in xs:
            to_x[a, k, o].wait_recv()
            passed[a, k, o].start()

    def complete(a, k):
        to_core[a, k].wait_recv()
        for o in xs:
            passed[a, k, o].wait_recv()

    hid_y, hid_z, hid_f = {}, {}, {}
    for s in range(n_x):
        for j in range(len(pieces)):
            here = hid[j].at[d, of_chip(s), :]
            hid_y[s, j] = remote(here, here, hy_s.at[s, j], hy_r.at[s, j], ypeer)
            for o in zs:
                hid_z[s, j, o] = remote(
                    here, here, hz_s.at[s, j, o - 1], hz_r.at[s, j, o - 1], z_to(o))
                there = hid[j].at[z_from(o), of_chip(s), :]
                hid_f[s, j, o] = remote(
                    there, there, hf_s.at[s, j, o - 1], hf_r.at[s, j, o - 1], ypeer)

    def pass_hidden(s, j):
        for o in zs:
            hid_z[s, j, o].wait_recv()
            hid_f[s, j, o].start()

    def forward(s, k):
        lhs = gt[of_chip(s), k * step:(k + 1) * step]
        for j, (f, n) in enumerate(pieces):
            fs, ks = slice(f, f + n), slice(k * step, (k + 1) * step)
            g = jnp.dot(lhs, wg[ks, fs], preferred_element_type=F32)
            u = jnp.dot(lhs, wu[ks, fs], preferred_element_type=F32)
            if k > 0:
                g, u = gate[of_chip(s), fs] + g, up[of_chip(s), fs] + u
            gate[of_chip(s), fs] = g
            up[of_chip(s), fs] = u
            if k == PARTS - 1:
                hid[j][d, of_chip(s), :] = (g * jax.nn.sigmoid(g) * u).astype(BF16)
                for o in zs:
                    hid_z[s, j, o].start()
                hid_y[s, j].start()

    own[0].wait()
    for k in range(PARTS):
        to_core[0, k].wait_recv()
        loads[k][0].wait()
        loads[k][1].wait()
        if k + 2 < PARTS:
            loads[k + 2][0].start()
            loads[k + 2][1].start()
        forward(0, k)
    for k in range(PARTS):
        arrive(0, k)
        for o in xs:
            to_x[1, k, o].start()
        loads[k][2].start()
        for o in xs:
            passed[0, k, o].wait_recv()
            forward(o, k)

    own[2].wait()
    for copy in exchange:
        copy.wait_recv()
    block = upc.at[:, of_tensor(t), :]
    up_core = remote(block, block, uc_s, uc_r, core)
    up_core.start()
    up_x, up_f = {}, {}
    for o in xs:
        up_x[o] = remote(block, block, ux_s.at[o - 1], ux_r.at[o - 1], x_to(o))
        there = upc.at[:, of_tensor(x_from(o)), :]
        up_f[o] = remote(there, there, uf_s.at[o - 1], uf_r.at[o - 1], core)

    own[1].wait()
    for k in range(PARTS):
        arrive(1, k)
        complete(1, k)
        loads[k][2].wait()
        ks = slice(k * step, (k + 1) * step)
        lhs = gu[:, ks]
        for f, n in pieces:
            fs = slice(f, f + n)
            p = contract_cols(lhs, wd[fs, ks])
            if k > 0:
                p = gh[:, fs] + p
            gh[:, fs] = p
        pass_hidden(0, k)
    for o in xs:
        up_x[o].start()
    for f, n in pieces:
        fs = slice(f, f + n)
        g, u = gate[:, fs], up[:, fs]
        h = gh[:, fs].astype(BF16).astype(F32)
        sig = jax.nn.sigmoid(g)
        gboth[:, fs] = (h * u * sig * (1.0 + g * (1.0 - sig))).astype(BF16)
        gboth[:, units + f:units + f + n] = (h * (g * sig)).astype(BF16)

    swap, chip = {}, {}
    for q in range(PARTS):
        swap[q] = remote(
            pc_out.at[:, :, cut(q)], pc_in.at[:, :, cut(q)], pc_s.at[q], pc_r.at[q], core)
        for o in xs:
            chip[q, o] = remote(
                cs_out.at[o - 1, :, cut(q)], cs_in.at[o - 1, :, cut(q)],
                cs_s.at[q, o - 1], cs_r.at[q, o - 1], x_to(o))

    def add_cores(q):
        swap[q].wait_recv()
        qs = slice(q * step, (q + 1) * step)
        for o in xs:
            to = lax.rem(x + o, n_x)
            both = part[of_tensor(to * 2 + c), qs] + pc_in[to, :, qs].astype(F32)
            cs_out[o - 1, :, qs] = both.astype(BF16)
            chip[q, o].start()

    for q in range(PARTS):
        qs = slice(q * step, (q + 1) * step)
        part[:, qs] = contract_cols(gboth[:, :units], wg[qs, :]) + contract_cols(
            gboth[:, units:], wu[qs, :])
        for i in range(n_x):
            pc_out[i, :, qs] = part[of_tensor(i * 2 + 1 - c), qs].astype(BF16)
        swap[q].start()
        if q > 0:
            add_cores(q - 1)
        if q == 2:
            pass_hidden(1, 0)
    add_cores(PARTS - 1)
    pass_hidden(1, 1)
    for o in xs:
        up_x[o].wait_recv()
        up_f[o].start()
    for q in range(PARTS):
        qs = slice(q * step, (q + 1) * step)
        total = part[of_tensor(t), qs] + pc_in[x, :, qs].astype(F32)
        for o in xs:
            chip[q, o].wait_recv()
            total = total + cs_in[o - 1, :, qs].astype(F32)
        gtok[:, qs] = total.astype(BF16)
    results = [pltpu.make_async_copy(gtok, gtok_h, out_sem.at[len(pieces)])]
    results[0].start()

    up_core.wait_recv()
    for o in xs:
        up_f[o].wait_recv()
    factor = float(n_dp * replica) ** (-0.5)
    pending = [(s, j) for s in range(n_x) for j in range(len(pieces))]
    pending = [p for p in pending if p not in ((0, 0), (0, 1), (0, 2), (0, 3), (1, 0), (1, 1))]
    for p in pending[:1]:
        pass_hidden(*p)
    for j, (f, n) in enumerate(pieces):
        if j == 1:
            for p in pending[1:]:
                pass_hidden(*p)
        for s in range(n_x):
            hid_y[s, j].wait_recv()
            for o in zs:
                hid_f[s, j, o].wait_recv()
        fs = slice(f, f + n)
        gdown[fs, :] = contract_rows(
            hid[j][...].reshape(n_dp * replica, n), upc[...].reshape(n_dp * replica, mine)
        ) * factor
        copy = pltpu.make_async_copy(
            gdown.at[pl.ds(f, n), :], gdown_h.at[pl.ds(f, n), :], out_sem.at[j])
        copy.start()
        results.append(copy)

    sent = [*to_core.values(), *to_x.values(), *passed.values(), *exchange, up_core,
            *up_x.values(), *up_f.values(), *hid_y.values(), *hid_z.values(), *hid_f.values(),
            *swap.values(), *chip.values()]
    for copy in sent:
        copy.wait_send()
    for copy in results:
        copy.wait()


PLACED = 8


def place(tokens_in, down_in, tokens_out, down_out, sem):
    part = down_in.shape[0] // PLACED
    copies = [pltpu.make_async_copy(tokens_in, tokens_out, sem.at[PLACED])]
    for i in range(PLACED):
        at = pl.ds(i * part, part)
        copies.append(pltpu.make_async_copy(down_in.at[at, :], down_out.at[at, :], sem.at[i]))
    for copy in copies:
        copy.start()
    for copy in copies:
        copy.wait()


def body(tokens, upstream_grad, w_gate, w_up, w_down):
    n_dp, n_tensor = lax.axis_size("dp"), lax.axis_size("tensor")
    rows, width = tokens.shape
    units = w_gate.shape[1]
    mine = width // n_dp
    n_x, n_z = n_tensor // 2, n_dp // 2
    if rows % 16 or n_tensor % 2 or n_dp % 2 or n_x != 2 or n_z < 2 or len(range(0, units, UNITS)) != PARTS:
        return plain_body(tokens, upstream_grad, w_gate, w_up, w_down)
    replica = rows * n_tensor
    n_pieces = -(-units // UNITS)
    dma = pltpu.SemaphoreType.DMA
    vmem = pltpu.VMEM

    def pair(*shape):
        return [dma(shape), dma(shape)] if shape else [dma, dma]

    scratch = [
        vmem((width, units), BF16), vmem((width, units), BF16), vmem((units, width), BF16),
        vmem((replica, width), BF16), vmem((replica, width), BF16),
        vmem((replica, units), F32), vmem((replica, units), F32), vmem((replica, units), F32),
        vmem((replica, 2 * units), BF16),
        [vmem((n_dp, replica, min(UNITS, units - f)), BF16) for f in range(0, units, UNITS)],
        vmem((n_dp, replica, mine), BF16),
        vmem((replica, width), F32),
        vmem((n_x, rows, width), BF16), vmem((n_x, rows, width), BF16),
        vmem((n_x - 1, rows, width), BF16), vmem((n_x - 1, rows, width), BF16),
        vmem((rows, width), BF16), vmem((units, mine), F32),
        dma((3, PARTS)), dma((3,)), dma((n_pieces + 1,)),
        *pair(2, PARTS), *pair(2, PARTS, n_x - 1), *pair(2, PARTS, n_x - 1),
        *pair(n_dp - 1), *pair(), *pair(n_x - 1), *pair(n_x - 1),
        *pair(n_x, n_pieces), *pair(n_x, n_pieces, n_z - 1), *pair(n_x, n_pieces, n_z - 1),
        *pair(PARTS), *pair(PARTS, n_x - 1),
    ]
    grads = pl.pallas_call(
        functools.partial(kernel, n_dp, n_tensor),
        out_shape=(
            jax.ShapeDtypeStruct((rows, width), BF16),
            jax.ShapeDtypeStruct((units, mine), F32),
        ),
        in_specs=[pl.BlockSpec(memory_space=pl.ANY)] * 5,
        out_specs=(pl.BlockSpec(memory_space=pl.ANY),) * 2,
        scratch_shapes=scratch,
        compiler_params=pltpu.CompilerParams(
            collective_id=0, has_side_effects=True, vmem_limit_bytes=56 * 1024 * 1024
        ),
        cost_estimate=pl.CostEstimate(
            flops=2 * replica * width * units * 6, bytes_accessed=6 * width * units,
            transcendentals=replica * units,
        ),
    )(tokens, upstream_grad, w_gate, w_up, w_down)
    return pl.pallas_call(
        place,
        out_shape=tuple(jax.ShapeDtypeStruct(g.shape, g.dtype) for g in grads),
        in_specs=[pl.BlockSpec(memory_space=pltpu.HBM)] * 2,
        out_specs=(pl.BlockSpec(memory_space=pltpu.HBM),) * 2,
        scratch_shapes=[dma((PLACED + 1,))],
    )(*grads)


def solution(mesh):
    in_specs = (
        P(("dp", "tensor"), None),
        P(("dp", "tensor"), None),
        P(None, "tensor"),
        P(None, "tensor"),
        P("tensor", None),
    )
    out_specs = (P(("dp", "tensor"), None), P("tensor", "dp"))
    return jax.shard_map(body, mesh=mesh, in_specs=in_specs, out_specs=out_specs, check_vma=False)
```

```python
import functools

import jax
import jax.numpy as jnp
from jax import lax
from jax.experimental import pallas as pl
from jax.experimental.pallas import tpu as pltpu
from jax.sharding import PartitionSpec as P


def contract_rows(left, right):
    return lax.dot_general(
        left, right, (((0,), (0,)), ((), ())), preferred_element_type=jnp.float32
    )


def contract_cols(left, right):
    return lax.dot_general(
        left, right, (((1,), (1,)), ((), ())), preferred_element_type=jnp.float32
    )


def plain_body(tokens, upstream_grad, w_gate, w_up, w_down):
    n_dp = lax.axis_size("dp")
    rows, width = upstream_grad.shape
    gathered = lax.all_gather(tokens, "tensor", axis=0, tiled=True)
    upstream = lax.all_gather(upstream_grad, "tensor", axis=0, tiled=True)
    mine = lax.all_to_all(
        upstream_grad.reshape(rows, n_dp, width // n_dp), "dp", split_axis=1, concat_axis=0
    )
    mine = lax.all_gather(mine.reshape(n_dp, rows, width // n_dp), "tensor", axis=1, tiled=True)
    mine = mine.reshape(-1, width // n_dp)
    gate_pre = jnp.dot(gathered, w_gate, preferred_element_type=jnp.float32)
    up_pre = jnp.dot(gathered, w_up, preferred_element_type=jnp.float32)
    sig_gate = jax.nn.sigmoid(gate_pre)
    act_gate = gate_pre * sig_gate
    hidden = (act_gate * up_pre).astype(jnp.bfloat16)
    hidden_all = lax.all_gather(hidden, "dp", axis=0, tiled=True)
    grad_hidden = contract_cols(upstream, w_down).astype(jnp.bfloat16)
    hidden_f = grad_hidden.astype(jnp.float32)
    grad_gate = (hidden_f * up_pre * sig_gate * (1.0 + gate_pre * (1.0 - sig_gate))).astype(
        jnp.bfloat16
    )
    grad_up = (hidden_f * act_gate).astype(jnp.bfloat16)
    factor = float(hidden_all.shape[0]) ** (-0.5)
    summed = lax.psum_scatter(
        (contract_cols(grad_gate, w_gate) + contract_cols(grad_up, w_up)).astype(jnp.bfloat16),
        "tensor",
        scatter_dimension=0,
        tiled=True,
    )
    grad_down = contract_rows(hidden_all, mine) * factor
    return (summed, grad_down)


MESH = pl.DeviceIdType.MESH
BF16 = jnp.bfloat16
F32 = jnp.float32
PARTS = 4
UNITS = 256


def kernel(
    n_dp, n_tensor,
    tok, upg, wg_h, wu_h, wd_h,
    gtok_h, gdown_h,
    wg, wu, wd, gt, gu, gate, up, gh, gboth, hid, upc, part, pc_out, pc_in, cs_out, cs_in,
    gtok, gdown,
    w_sem, loc_sem, out_sem,
    core_s, core_r, x_s, x_r, fwd_s, fwd_r,
    a2a_s, a2a_r, uc_s, uc_r, ux_s, ux_r, uf_s, uf_r,
    hy_s, hy_r, hz_s, hz_r, hf_s, hf_r,
    pc_s, pc_r, cs_s, cs_r,
):
    rows, width = tok.shape
    units = wg_h.shape[1]
    replica = rows * n_tensor
    step = width // PARTS
    mine = width // n_dp
    n_x, n_z = n_tensor // 2, n_dp // 2
    d, t = lax.axis_index("dp"), lax.axis_index("tensor")
    c, x = lax.rem(t, 2), lax.div(t, 2)
    y, z = lax.rem(d, 2), lax.div(d, 2)
    core = (d, x * 2 + 1 - c)
    ypeer = (z * 2 + 1 - y, t)
    xs, zs = range(1, n_x), range(1, n_z)
    pieces = [(f, min(UNITS, units - f)) for f in range(0, units, UNITS)]

    def x_to(o):
        return (d, lax.rem(x + o, n_x) * 2 + c)

    def x_from(o):
        return lax.rem(x + n_x - o, n_x) * 2 + c

    def z_to(o):
        return (lax.rem(z + o, n_z) * 2 + y, t)

    def z_from(o):
        return lax.rem(z + n_z - o, n_z) * 2 + y

    def dp_to(o):
        return lax.rem(d + o, n_dp)

    def of_tensor(i):
        return pl.ds(pl.multiple_of(i * rows, rows), rows)

    def of_chip(o):
        return pl.ds(pl.multiple_of(lax.rem(x + n_x - o, n_x) * 2 * rows, 2 * rows), 2 * rows)

    def cut(k):
        return pl.ds(k * step, step)

    def remote(src, dst, s, r, to):
        return pltpu.make_async_remote_copy(
            src_ref=src, dst_ref=dst, send_sem=s, recv_sem=r, device_id=to, device_id_type=MESH
        )

    loads = [[
        pltpu.make_async_copy(wg_h.at[cut(k), :], wg.at[cut(k), :], w_sem.at[0, k]),
        pltpu.make_async_copy(wu_h.at[cut(k), :], wu.at[cut(k), :], w_sem.at[1, k]),
        pltpu.make_async_copy(wd_h.at[:, cut(k)], wd.at[:, cut(k)], w_sem.at[2, k]),
    ] for k in range(PARTS)]
    own = [
        pltpu.make_async_copy(tok, gt.at[of_tensor(t), :], loc_sem.at[0]),
        pltpu.make_async_copy(upg, gu.at[of_tensor(t), :], loc_sem.at[1]),
        pltpu.make_async_copy(
            upg.at[:, pl.ds(pl.multiple_of(d * mine, mine), mine)],
            upc.at[d, of_tensor(t), :], loc_sem.at[2]),
    ]
    for copy in own:
        copy.start()
    for k in range(2):
        loads[k][0].start()
        loads[k][1].start()

    barrier = pltpu.get_barrier_semaphore()
    pl.semaphore_signal(barrier, inc=1, device_id=core, device_id_type=MESH)
    for o in xs:
        pl.semaphore_signal(barrier, inc=1, device_id=x_to(o), device_id_type=MESH)
    for o in range(1, n_dp):
        pl.semaphore_signal(barrier, inc=1, device_id=(dp_to(o), t), device_id_type=MESH)
    pl.semaphore_wait(barrier, 1 + (n_x - 1) + (n_dp - 1))
    own[0].wait()
    own[1].wait()

    to_core, to_x, passed = {}, {}, {}
    for a, all_rows in enumerate((gt, gu)):
        for k in range(PARTS):
            here = all_rows.at[of_tensor(t), cut(k)]
            to_core[a, k] = remote(
                here, here,
                core_s.at[a, k], core_r.at[a, k], core)
            for o in xs:
                to_x[a, k, o] = remote(
                    here, here,
                    x_s.at[a, k, o - 1], x_r.at[a, k, o - 1], x_to(o))
                there = all_rows.at[of_tensor(x_from(o)), cut(k)]
                passed[a, k, o] = remote(
                    there, there, fwd_s.at[a, k, o - 1], fwd_r.at[a, k, o - 1], core)
    for k in range(PARTS):
        for o in xs:
            to_x[0, k, o].start()
        to_core[0, k].start()
    exchange = [
        remote(
            gu.at[of_tensor(t), pl.ds(pl.multiple_of(dp_to(o) * mine, mine), mine)],
            upc.at[d, of_tensor(t), :],
            a2a_s.at[o - 1], a2a_r.at[o - 1], (dp_to(o), t))
        for o in range(1, n_dp)
    ]
    for copy in exchange:
        copy.start()
    for k in range(PARTS):
        to_core[1, k].start()

    def arrive(a, k):
        for o in xs:
            to_x[a, k, o].wait_recv()
            passed[a, k, o].start()

    def complete(a, k):
        to_core[a, k].wait_recv()
        for o in xs:
            passed[a, k, o].wait_recv()

    hid_y, hid_z, hid_f = {}, {}, {}
    for s in range(n_x):
        for j in range(len(pieces)):
            here = hid[j].at[d, of_chip(s), :]
            hid_y[s, j] = remote(here, here, hy_s.at[s, j], hy_r.at[s, j], ypeer)
            for o in zs:
                hid_z[s, j, o] = remote(
                    here, here, hz_s.at[s, j, o - 1], hz_r.at[s, j, o - 1], z_to(o))
                there = hid[j].at[z_from(o), of_chip(s), :]
                hid_f[s, j, o] = remote(
                    there, there, hf_s.at[s, j, o - 1], hf_r.at[s, j, o - 1], ypeer)

    def pass_hidden(s, j):
        for o in zs:
            hid_z[s, j, o].wait_recv()
            hid_f[s, j, o].start()

    def forward(s, k):
        lhs = gt[of_chip(s), k * step:(k + 1) * step]
        for j, (f, n) in enumerate(pieces):
            fs, ks = slice(f, f + n), slice(k * step, (k + 1) * step)
            g = jnp.dot(lhs, wg[ks, fs], preferred_element_type=F32)
            u = jnp.dot(lhs, wu[ks, fs], preferred_element_type=F32)
            if k > 0:
                g, u = gate[of_chip(s), fs] + g, up[of_chip(s), fs] + u
            gate[of_chip(s), fs] = g
            up[of_chip(s), fs] = u
            if k == PARTS - 1:
                hid[j][d, of_chip(s), :] = (g * jax.nn.sigmoid(g) * u).astype(BF16)
                for o in zs:
                    hid_z[s, j, o].start()
                hid_y[s, j].start()

    for k in range(PARTS):
        to_core[0, k].wait_recv()
        loads[k][0].wait()
        loads[k][1].wait()
        if k + 2 < PARTS:
            loads[k + 2][0].start()
            loads[k + 2][1].start()
        forward(0, k)
    for k in range(PARTS):
        arrive(0, k)
        for o in xs:
            to_x[1, k, o].start()
        loads[k][2].start()
        for o in xs:
            passed[0, k, o].wait_recv()
            forward(o, k)

    own[2].wait()
    for copy in exchange:
        copy.wait_recv()
    block = upc.at[:, of_tensor(t), :]
    up_core = remote(block, block, uc_s, uc_r, core)
    up_core.start()
    up_x, up_f = {}, {}
    for o in xs:
        up_x[o] = remote(block, block, ux_s.at[o - 1], ux_r.at[o - 1], x_to(o))
        there = upc.at[:, of_tensor(x_from(o)), :]
        up_f[o] = remote(there, there, uf_s.at[o - 1], uf_r.at[o - 1], core)

    for k in range(PARTS):
        arrive(1, k)
        complete(1, k)
        loads[k][2].wait()
        ks = slice(k * step, (k + 1) * step)
        lhs = gu[:, ks]
        for f, n in pieces:
            fs = slice(f, f + n)
            p = contract_cols(wd[fs, ks], lhs)
            if k > 0:
                p = gh[fs, :] + p
            gh[fs, :] = p
        pass_hidden(0, k)
    for o in xs:
        up_x[o].start()
    for f, n in pieces:
        fs = slice(f, f + n)
        g, u = gate[:, fs], up[:, fs]
        h = gh[fs, :].T.astype(BF16).astype(F32)
        sig = jax.nn.sigmoid(g)
        gboth[:, fs] = (h * u * sig * (1.0 + g * (1.0 - sig))).astype(BF16)
        gboth[:, units + f:units + f + n] = (h * (g * sig)).astype(BF16)

    swap, chip = {}, {}
    for q in range(PARTS):
        swap[q] = remote(
            pc_out.at[:, :, cut(q)], pc_in.at[:, :, cut(q)], pc_s.at[q], pc_r.at[q], core)
        for o in xs:
            chip[q, o] = remote(
                cs_out.at[o - 1, :, cut(q)], cs_in.at[o - 1, :, cut(q)],
                cs_s.at[q, o - 1], cs_r.at[q, o - 1], x_to(o))

    def add_cores(q):
        swap[q].wait_recv()
        qs = slice(q * step, (q + 1) * step)
        for o in xs:
            to = lax.rem(x + o, n_x)
            both = part[of_tensor(to * 2 + c), qs] + pc_in[to, :, qs].astype(F32)
            cs_out[o - 1, :, qs] = both.astype(BF16)
            chip[q, o].start()

    for q in range(PARTS):
        qs = slice(q * step, (q + 1) * step)
        both = contract_cols(wg[qs, :], gboth[:, :units]) + contract_cols(
            wu[qs, :], gboth[:, units:])
        part[:, qs] = both.T
        for i in range(n_x):
            pc_out[i, :, qs] = part[of_tensor(i * 2 + 1 - c), qs].astype(BF16)
        swap[q].start()
        if q > 0:
            add_cores(q - 1)
        if q == 2:
            pass_hidden(1, 0)
    add_cores(PARTS - 1)
    pass_hidden(1, 1)
    for o in xs:
        up_x[o].wait_recv()
        up_f[o].start()
    for q in range(PARTS):
        qs = slice(q * step, (q + 1) * step)
        total = part[of_tensor(t), qs] + pc_in[x, :, qs].astype(F32)
        for o in xs:
            chip[q, o].wait_recv()
            total = total + cs_in[o - 1, :, qs].astype(F32)
        gtok[:, qs] = total.astype(BF16)
    results = [pltpu.make_async_copy(gtok, gtok_h, out_sem.at[len(pieces)])]
    results[0].start()

    up_core.wait_recv()
    for o in xs:
        up_f[o].wait_recv()
    factor = float(n_dp * replica) ** (-0.5)
    pending = [(s, j) for s in range(n_x) for j in range(len(pieces))]
    pending = [p for p in pending if p not in ((0, 0), (0, 1), (0, 2), (0, 3), (1, 0), (1, 1))]
    for p in pending[:1]:
        pass_hidden(*p)
    for j, (f, n) in enumerate(pieces):
        if j == 1:
            for p in pending[1:]:
                pass_hidden(*p)
        for s in range(n_x):
            hid_y[s, j].wait_recv()
            for o in zs:
                hid_f[s, j, o].wait_recv()
        fs = slice(f, f + n)
        gdown[fs, :] = contract_rows(
            hid[j][...].reshape(n_dp * replica, n), upc[...].reshape(n_dp * replica, mine)
        ) * factor
        copy = pltpu.make_async_copy(
            gdown.at[pl.ds(f, n), :], gdown_h.at[pl.ds(f, n), :], out_sem.at[j])
        copy.start()
        results.append(copy)

    sent = [*to_core.values(), *to_x.values(), *passed.values(), *exchange, up_core,
            *up_x.values(), *up_f.values(), *hid_y.values(), *hid_z.values(), *hid_f.values(),
            *swap.values(), *chip.values()]
    for copy in sent:
        copy.wait_send()
    for copy in results:
        copy.wait()


PLACED = 4


def place(tokens_in, down_in, tokens_out, down_out, tokens_held, down_held, read, written):
    n = down_in.shape[0] // PLACED
    moves = [(tokens_in, tokens_held, tokens_out)]
    for i in range(PLACED):
        at = pl.ds(i * n, n)
        moves.append((down_in.at[at, :], down_held.at[at, :], down_out.at[at, :]))
    ins = [pltpu.make_async_copy(a, b, read.at[i]) for i, (a, b, _) in enumerate(moves)]
    outs = [pltpu.make_async_copy(b, c, written.at[i]) for i, (_, b, c) in enumerate(moves)]
    for copy in ins:
        copy.start()
    for copy, then in zip(ins, outs):
        copy.wait()
        then.start()
    for copy in outs:
        copy.wait()


def body(tokens, upstream_grad, w_gate, w_up, w_down):
    n_dp, n_tensor = lax.axis_size("dp"), lax.axis_size("tensor")
    rows, width = tokens.shape
    units = w_gate.shape[1]
    mine = width // n_dp
    n_x, n_z = n_tensor // 2, n_dp // 2
    if rows % 16 or n_tensor % 2 or n_dp % 2 or n_x != 2 or n_z < 2 or len(range(0, units, UNITS)) != PARTS:
        return plain_body(tokens, upstream_grad, w_gate, w_up, w_down)
    replica = rows * n_tensor
    n_pieces = -(-units // UNITS)
    dma = pltpu.SemaphoreType.DMA
    vmem = pltpu.VMEM

    def pair(*shape):
        return [dma(shape), dma(shape)] if shape else [dma, dma]

    scratch = [
        vmem((width, units), BF16), vmem((width, units), BF16), vmem((units, width), BF16),
        vmem((replica, width), BF16), vmem((replica, width), BF16),
        vmem((replica, units), F32), vmem((replica, units), F32), vmem((units, replica), F32),
        vmem((replica, 2 * units), BF16),
        [vmem((n_dp, replica, min(UNITS, units - f)), BF16) for f in range(0, units, UNITS)],
        vmem((n_dp, replica, mine), BF16),
        vmem((replica, width), F32),
        vmem((n_x, rows, width), BF16), vmem((n_x, rows, width), BF16),
        vmem((n_x - 1, rows, width), BF16), vmem((n_x - 1, rows, width), BF16),
        vmem((rows, width), BF16), vmem((units, mine), F32),
        dma((3, PARTS)), dma((3,)), dma((n_pieces + 1,)),
        *pair(2, PARTS), *pair(2, PARTS, n_x - 1), *pair(2, PARTS, n_x - 1),
        *pair(n_dp - 1), *pair(), *pair(n_x - 1), *pair(n_x - 1),
        *pair(n_x, n_pieces), *pair(n_x, n_pieces, n_z - 1), *pair(n_x, n_pieces, n_z - 1),
        *pair(PARTS), *pair(PARTS, n_x - 1),
    ]
    grads = pl.pallas_call(
        functools.partial(kernel, n_dp, n_tensor),
        out_shape=(
            jax.ShapeDtypeStruct((rows, width), BF16),
            jax.ShapeDtypeStruct((units, mine), F32),
        ),
        in_specs=[pl.BlockSpec(memory_space=pl.ANY)] * 5,
        out_specs=(pl.BlockSpec(memory_space=pl.ANY),) * 2,
        scratch_shapes=scratch,
        compiler_params=pltpu.CompilerParams(
            collective_id=0, has_side_effects=True, vmem_limit_bytes=56 * 1024 * 1024
        ),
        cost_estimate=pl.CostEstimate(
            flops=2 * replica * width * units * 6, bytes_accessed=6 * width * units,
            transcendentals=replica * units,
        ),
    )(tokens, upstream_grad, w_gate, w_up, w_down)
    return pl.pallas_call(
        place,
        out_shape=tuple(jax.ShapeDtypeStruct(g.shape, g.dtype) for g in grads),
        in_specs=[pl.BlockSpec(memory_space=pltpu.HBM)] * 2,
        out_specs=(pl.BlockSpec(memory_space=pltpu.HBM),) * 2,
        scratch_shapes=[
            vmem((rows, width), BF16), vmem((units, mine), F32),
            dma((PLACED + 1,)), dma((PLACED + 1,)),
        ],
    )(*grads)


def solution(mesh):
    in_specs = (
        P(("dp", "tensor"), None),
        P(("dp", "tensor"), None),
        P(None, "tensor"),
        P(None, "tensor"),
        P("tensor", None),
    )
    out_specs = (P(("dp", "tensor"), None), P("tensor", "dp"))
    return jax.shard_map(body, mesh=mesh, in_specs=in_specs, out_specs=out_specs, check_vma=False)
```

```python
import functools

import jax
import jax.numpy as jnp
from jax import lax
from jax.experimental import pallas as pl
from jax.experimental.pallas import tpu as pltpu
from jax.sharding import PartitionSpec as P


def contract_rows(left, right):
    return lax.dot_general(
        left, right, (((0,), (0,)), ((), ())), preferred_element_type=jnp.float32
    )


def contract_cols(left, right):
    return lax.dot_general(
        left, right, (((1,), (1,)), ((), ())), preferred_element_type=jnp.float32
    )


def plain_body(tokens, upstream_grad, w_gate, w_up, w_down):
    n_dp = lax.axis_size("dp")
    rows, width = upstream_grad.shape
    gathered = lax.all_gather(tokens, "tensor", axis=0, tiled=True)
    upstream = lax.all_gather(upstream_grad, "tensor", axis=0, tiled=True)
    mine = lax.all_to_all(
        upstream_grad.reshape(rows, n_dp, width // n_dp), "dp", split_axis=1, concat_axis=0
    )
    mine = lax.all_gather(mine.reshape(n_dp, rows, width // n_dp), "tensor", axis=1, tiled=True)
    mine = mine.reshape(-1, width // n_dp)
    gate_pre = jnp.dot(gathered, w_gate, preferred_element_type=jnp.float32)
    up_pre = jnp.dot(gathered, w_up, preferred_element_type=jnp.float32)
    sig_gate = jax.nn.sigmoid(gate_pre)
    act_gate = gate_pre * sig_gate
    hidden = (act_gate * up_pre).astype(jnp.bfloat16)
    hidden_all = lax.all_gather(hidden, "dp", axis=0, tiled=True)
    grad_hidden = contract_cols(upstream, w_down).astype(jnp.bfloat16)
    hidden_f = grad_hidden.astype(jnp.float32)
    grad_gate = (hidden_f * up_pre * sig_gate * (1.0 + gate_pre * (1.0 - sig_gate))).astype(
        jnp.bfloat16
    )
    grad_up = (hidden_f * act_gate).astype(jnp.bfloat16)
    factor = float(hidden_all.shape[0]) ** (-0.5)
    summed = lax.psum_scatter(
        (contract_cols(grad_gate, w_gate) + contract_cols(grad_up, w_up)).astype(jnp.bfloat16),
        "tensor",
        scatter_dimension=0,
        tiled=True,
    )
    grad_down = contract_rows(hidden_all, mine) * factor
    return (summed, grad_down)


MESH = pl.DeviceIdType.MESH
BF16 = jnp.bfloat16
F32 = jnp.float32
PARTS = 4
UNITS = 256


def kernel(
    n_dp, n_tensor,
    tok, upg, wg_h, wu_h, wd_h,
    gtok_h, gdown_h,
    wg, wu, wd, gt, gu, gate, up, gh, gboth, hid, upc, part, pc_out, pc_in, cs_out, cs_in,
    gtok, gdown,
    w_sem, loc_sem, out_sem,
    core_s, core_r, x_s, x_r, fwd_s, fwd_r,
    a2a_s, a2a_r, uc_s, uc_r, ux_s, ux_r, uf_s, uf_r,
    hy_s, hy_r, hz_s, hz_r, hf_s, hf_r,
    pc_s, pc_r, cs_s, cs_r,
):
    rows, width = tok.shape
    units = wg_h.shape[1]
    replica = rows * n_tensor
    step = width // PARTS
    mine = width // n_dp
    n_x, n_z = n_tensor // 2, n_dp // 2
    d, t = lax.axis_index("dp"), lax.axis_index("tensor")
    c, x = lax.rem(t, 2), lax.div(t, 2)
    y, z = lax.rem(d, 2), lax.div(d, 2)
    core = (d, x * 2 + 1 - c)
    ypeer = (z * 2 + 1 - y, t)
    xs, zs = range(1, n_x), range(1, n_z)
    pieces = [(f, min(UNITS, units - f)) for f in range(0, units, UNITS)]

    def x_to(o):
        return (d, lax.rem(x + o, n_x) * 2 + c)

    def x_from(o):
        return lax.rem(x + n_x - o, n_x) * 2 + c

    def z_from(o):
        partner = (z + 1 - 2 * lax.rem(z, 2), lax.rem(z + 2, 4), 3 - z)[o - 1]
        return partner * 2 + y

    def z_to(o):
        return (z_from(o), t)

    def dp_to(o):
        return lax.rem(d + o, n_dp)

    def of_tensor(i):
        return pl.ds(pl.multiple_of(i * rows, rows), rows)

    def of_chip(o):
        return pl.ds(pl.multiple_of(lax.rem(x + n_x - o, n_x) * 2 * rows, 2 * rows), 2 * rows)

    def cut(k):
        return pl.ds(k * step, step)

    def remote(src, dst, s, r, to):
        return pltpu.make_async_remote_copy(
            src_ref=src, dst_ref=dst, send_sem=s, recv_sem=r, device_id=to, device_id_type=MESH
        )

    loads = [[
        pltpu.make_async_copy(wg_h.at[cut(k), :], wg.at[cut(k), :], w_sem.at[0, k]),
        pltpu.make_async_copy(wu_h.at[cut(k), :], wu.at[cut(k), :], w_sem.at[1, k]),
        pltpu.make_async_copy(wd_h.at[:, cut(k)], wd.at[:, cut(k)], w_sem.at[2, k]),
    ] for k in range(PARTS)]
    own = [
        pltpu.make_async_copy(tok, gt.at[of_tensor(t), :], loc_sem.at[0]),
        pltpu.make_async_copy(upg, gu.at[of_tensor(t), :], loc_sem.at[1]),
        pltpu.make_async_copy(
            upg.at[:, pl.ds(pl.multiple_of(d * mine, mine), mine)],
            upc.at[d, of_tensor(t), :], loc_sem.at[2]),
    ]
    for copy in own:
        copy.start()
    for k in range(2):
        loads[k][0].start()
        loads[k][1].start()

    barrier = pltpu.get_barrier_semaphore()
    pl.semaphore_signal(barrier, inc=1, device_id=core, device_id_type=MESH)
    for o in xs:
        pl.semaphore_signal(barrier, inc=1, device_id=x_to(o), device_id_type=MESH)
    for o in range(1, n_dp):
        pl.semaphore_signal(barrier, inc=1, device_id=(dp_to(o), t), device_id_type=MESH)
    pl.semaphore_wait(barrier, 1 + (n_x - 1) + (n_dp - 1))
    own[0].wait()
    own[1].wait()

    to_core, to_x, passed = {}, {}, {}
    for a, all_rows in enumerate((gt, gu)):
        for k in range(PARTS):
            here = all_rows.at[of_tensor(t), cut(k)]
            to_core[a, k] = remote(
                here, here,
                core_s.at[a, k], core_r.at[a, k], core)
            for o in xs:
                to_x[a, k, o] = remote(
                    here, here,
                    x_s.at[a, k, o - 1], x_r.at[a, k, o - 1], x_to(o))
                there = all_rows.at[of_tensor(x_from(o)), cut(k)]
                passed[a, k, o] = remote(
                    there, there, fwd_s.at[a, k, o - 1], fwd_r.at[a, k, o - 1], core)
    for k in range(PARTS):
        for o in xs:
            to_x[0, k, o].start()
        to_core[0, k].start()
    exchange = [
        remote(
            gu.at[of_tensor(t), pl.ds(pl.multiple_of(dp_to(o) * mine, mine), mine)],
            upc.at[d, of_tensor(t), :],
            a2a_s.at[o - 1], a2a_r.at[o - 1], (dp_to(o), t))
        for o in range(1, n_dp)
    ]
    for copy in exchange:
        copy.start()
    for k in range(PARTS):
        to_core[1, k].start()

    def arrive(a, k):
        for o in xs:
            to_x[a, k, o].wait_recv()
            passed[a, k, o].start()

    def complete(a, k):
        to_core[a, k].wait_recv()
        for o in xs:
            passed[a, k, o].wait_recv()

    hid_y, hid_z, hid_f = {}, {}, {}
    for s in range(n_x):
        for j in range(len(pieces)):
            here = hid[j].at[d, of_chip(s), :]
            hid_y[s, j] = remote(here, here, hy_s.at[s, j], hy_r.at[s, j], ypeer)
            for o in zs:
                hid_z[s, j, o] = remote(
                    here, here, hz_s.at[s, j, o - 1], hz_r.at[s, j, o - 1], z_to(o))
                there = hid[j].at[z_from(o), of_chip(s), :]
                hid_f[s, j, o] = remote(
                    there, there, hf_s.at[s, j, o - 1], hf_r.at[s, j, o - 1], ypeer)

    def pass_hidden(s, j):
        for o in zs:
            hid_z[s, j, o].wait_recv()
            hid_f[s, j, o].start()

    def forward(s, k):
        lhs = gt[of_chip(s), k * step:(k + 1) * step]
        for j, (f, n) in enumerate(pieces):
            fs, ks = slice(f, f + n), slice(k * step, (k + 1) * step)
            g = jnp.dot(lhs, wg[ks, fs], preferred_element_type=F32)
            u = jnp.dot(lhs, wu[ks, fs], preferred_element_type=F32)
            if k > 0:
                g, u = gate[of_chip(s), fs] + g, up[of_chip(s), fs] + u
            gate[of_chip(s), fs] = g
            up[of_chip(s), fs] = u
            if k == PARTS - 1:
                hid[j][d, of_chip(s), :] = (g * jax.nn.sigmoid(g) * u).astype(BF16)
                for o in zs:
                    hid_z[s, j, o].start()
                hid_y[s, j].start()

    for k in range(PARTS):
        to_core[0, k].wait_recv()
        loads[k][0].wait()
        loads[k][1].wait()
        if k + 2 < PARTS:
            loads[k + 2][0].start()
            loads[k + 2][1].start()
        forward(0, k)
    for k in range(PARTS):
        arrive(0, k)
        for o in xs:
            to_x[1, k, o].start()
        loads[k][2].start()
        for o in xs:
            passed[0, k, o].wait_recv()
            forward(o, k)

    own[2].wait()
    for copy in exchange:
        copy.wait_recv()
    block = upc.at[:, of_tensor(t), :]
    up_core = remote(block, block, uc_s, uc_r, core)
    up_core.start()
    up_x, up_f = {}, {}
    for o in xs:
        up_x[o] = remote(block, block, ux_s.at[o - 1], ux_r.at[o - 1], x_to(o))
        there = upc.at[:, of_tensor(x_from(o)), :]
        up_f[o] = remote(there, there, uf_s.at[o - 1], uf_r.at[o - 1], core)

    for k in range(PARTS):
        arrive(1, k)
        complete(1, k)
        loads[k][2].wait()
        ks = slice(k * step, (k + 1) * step)
        lhs = gu[:, ks]
        for f, n in pieces:
            fs = slice(f, f + n)
            p = contract_cols(wd[fs, ks], lhs)
            if k > 0:
                p = gh[fs, :] + p
            gh[fs, :] = p
        if k >= 2:
            pass_hidden(0, k - 2)
    for o in xs:
        up_x[o].start()
    for f, n in pieces:
        fs = slice(f, f + n)
        g, u = gate[:, fs], up[:, fs]
        h = gh[fs, :].T.astype(BF16).astype(F32)
        sig = jax.nn.sigmoid(g)
        gboth[:, fs] = (h * u * sig * (1.0 + g * (1.0 - sig))).astype(BF16)
        gboth[:, units + f:units + f + n] = (h * (g * sig)).astype(BF16)

    swap, chip = {}, {}
    for q in range(PARTS):
        swap[q] = remote(
            pc_out.at[:, :, cut(q)], pc_in.at[:, :, cut(q)], pc_s.at[q], pc_r.at[q], core)
        for o in xs:
            chip[q, o] = remote(
                cs_out.at[o - 1, :, cut(q)], cs_in.at[o - 1, :, cut(q)],
                cs_s.at[q, o - 1], cs_r.at[q, o - 1], x_to(o))

    def add_cores(q):
        swap[q].wait_recv()
        qs = slice(q * step, (q + 1) * step)
        for o in xs:
            to = lax.rem(x + o, n_x)
            both = part[of_tensor(to * 2 + c), qs] + pc_in[to, :, qs].astype(F32)
            cs_out[o - 1, :, qs] = both.astype(BF16)
            chip[q, o].start()

    for q in range(PARTS):
        qs = slice(q * step, (q + 1) * step)
        both = contract_cols(wg[qs, :], gboth[:, :units]) + contract_cols(
            wu[qs, :], gboth[:, units:])
        part[:, qs] = both.T
        for i in range(n_x):
            pc_out[i, :, qs] = part[of_tensor(i * 2 + 1 - c), qs].astype(BF16)
        swap[q].start()
        if q > 0:
            add_cores(q - 1)
        if q == 2:
            pass_hidden(0, 2)
    add_cores(PARTS - 1)
    pass_hidden(0, 3)
    for o in xs:
        up_x[o].wait_recv()
        up_f[o].start()
    pass_hidden(1, 0)
    for q in range(PARTS):
        qs = slice(q * step, (q + 1) * step)
        total = part[of_tensor(t), qs] + pc_in[x, :, qs].astype(F32)
        for o in xs:
            chip[q, o].wait_recv()
            total = total + cs_in[o - 1, :, qs].astype(F32)
        gtok[:, qs] = total.astype(BF16)
    results = [pltpu.make_async_copy(gtok, gtok_h, out_sem.at[len(pieces)])]
    results[0].start()

    up_core.wait_recv()
    for o in xs:
        up_f[o].wait_recv()
    factor = float(n_dp * replica) ** (-0.5)
    pass_hidden(1, 1)
    for j, (f, n) in enumerate(pieces):
        if j == 0:
            pass_hidden(1, 2)
        if j == 1:
            pass_hidden(1, 3)
        for s in range(n_x):
            hid_y[s, j].wait_recv()
            for o in zs:
                hid_f[s, j, o].wait_recv()
        fs = slice(f, f + n)
        gdown[fs, :] = contract_rows(
            hid[j][...].reshape(n_dp * replica, n), upc[...].reshape(n_dp * replica, mine)
        ) * factor
        copy = pltpu.make_async_copy(
            gdown.at[pl.ds(f, n), :], gdown_h.at[pl.ds(f, n), :], out_sem.at[j])
        copy.start()
        results.append(copy)

    sent = [*to_core.values(), *to_x.values(), *passed.values(), *exchange, up_core,
            *up_x.values(), *up_f.values(), *hid_y.values(), *hid_z.values(), *hid_f.values(),
            *swap.values(), *chip.values()]
    for copy in sent:
        copy.wait_send()
    for copy in results:
        copy.wait()


PLACED = 4


def place(tokens_in, down_in, tokens_out, down_out, tokens_held, down_held, read, written):
    n = down_in.shape[0] // PLACED
    moves = [(tokens_in, tokens_held, tokens_out)]
    for i in range(PLACED):
        at = pl.ds(i * n, n)
        moves.append((down_in.at[at, :], down_held.at[at, :], down_out.at[at, :]))
    ins = [pltpu.make_async_copy(a, b, read.at[i]) for i, (a, b, _) in enumerate(moves)]
    outs = [pltpu.make_async_copy(b, c, written.at[i]) for i, (_, b, c) in enumerate(moves)]
    for copy in ins:
        copy.start()
    for copy, then in zip(ins, outs):
        copy.wait()
        then.start()
    for copy in outs:
        copy.wait()


def body(tokens, upstream_grad, w_gate, w_up, w_down):
    n_dp, n_tensor = lax.axis_size("dp"), lax.axis_size("tensor")
    rows, width = tokens.shape
    units = w_gate.shape[1]
    mine = width // n_dp
    n_x, n_z = n_tensor // 2, n_dp // 2
    if rows % 16 or n_tensor % 2 or n_dp % 2 or n_x != 2 or n_z != 4 or len(range(0, units, UNITS)) != PARTS:
        return plain_body(tokens, upstream_grad, w_gate, w_up, w_down)
    replica = rows * n_tensor
    n_pieces = -(-units // UNITS)
    dma = pltpu.SemaphoreType.DMA
    vmem = pltpu.VMEM

    def pair(*shape):
        return [dma(shape), dma(shape)] if shape else [dma, dma]

    scratch = [
        vmem((width, units), BF16), vmem((width, units), BF16), vmem((units, width), BF16),
        vmem((replica, width), BF16), vmem((replica, width), BF16),
        vmem((replica, units), F32), vmem((replica, units), F32), vmem((units, replica), F32),
        vmem((replica, 2 * units), BF16),
        [vmem((n_dp, replica, min(UNITS, units - f)), BF16) for f in range(0, units, UNITS)],
        vmem((n_dp, replica, mine), BF16),
        vmem((replica, width), F32),
        vmem((n_x, rows, width), BF16), vmem((n_x, rows, width), BF16),
        vmem((n_x - 1, rows, width), BF16), vmem((n_x - 1, rows, width), BF16),
        vmem((rows, width), BF16), vmem((units, mine), F32),
        dma((3, PARTS)), dma((3,)), dma((n_pieces + 1,)),
        *pair(2, PARTS), *pair(2, PARTS, n_x - 1), *pair(2, PARTS, n_x - 1),
        *pair(n_dp - 1), *pair(), *pair(n_x - 1), *pair(n_x - 1),
        *pair(n_x, n_pieces), *pair(n_x, n_pieces, n_z - 1), *pair(n_x, n_pieces, n_z - 1),
        *pair(PARTS), *pair(PARTS, n_x - 1),
    ]
    grads = pl.pallas_call(
        functools.partial(kernel, n_dp, n_tensor),
        out_shape=(
            jax.ShapeDtypeStruct((rows, width), BF16),
            jax.ShapeDtypeStruct((units, mine), F32),
        ),
        in_specs=[pl.BlockSpec(memory_space=pl.ANY)] * 5,
        out_specs=(pl.BlockSpec(memory_space=pl.ANY),) * 2,
        scratch_shapes=scratch,
        compiler_params=pltpu.CompilerParams(
            collective_id=0, has_side_effects=True, vmem_limit_bytes=56 * 1024 * 1024
        ),
        cost_estimate=pl.CostEstimate(
            flops=2 * replica * width * units * 6, bytes_accessed=6 * width * units,
            transcendentals=replica * units,
        ),
    )(tokens, upstream_grad, w_gate, w_up, w_down)
    return pl.pallas_call(
        place,
        out_shape=tuple(jax.ShapeDtypeStruct(g.shape, g.dtype) for g in grads),
        in_specs=[pl.BlockSpec(memory_space=pltpu.HBM)] * 2,
        out_specs=(pl.BlockSpec(memory_space=pltpu.HBM),) * 2,
        scratch_shapes=[
            vmem((rows, width), BF16), vmem((units, mine), F32),
            dma((PLACED + 1,)), dma((PLACED + 1,)),
        ],
    )(*grads)


def solution(mesh):
    in_specs = (
        P(("dp", "tensor"), None),
        P(("dp", "tensor"), None),
        P(None, "tensor"),
        P(None, "tensor"),
        P("tensor", None),
    )
    out_specs = (P(("dp", "tensor"), None), P("tensor", "dp"))
    return jax.shard_map(body, mesh=mesh, in_specs=in_specs, out_specs=out_specs, check_vma=False)
```

```python
import functools

import jax
import jax.numpy as jnp
from jax import lax
from jax.experimental import pallas as pl
from jax.experimental.pallas import tpu as pltpu
from jax.sharding import PartitionSpec as P


def contract_rows(left, right):
    return lax.dot_general(
        left, right, (((0,), (0,)), ((), ())), preferred_element_type=jnp.float32
    )


def contract_cols(left, right):
    return lax.dot_general(
        left, right, (((1,), (1,)), ((), ())), preferred_element_type=jnp.float32
    )


def plain_body(tokens, upstream_grad, w_gate, w_up, w_down):
    n_dp = lax.axis_size("dp")
    rows, width = upstream_grad.shape
    gathered = lax.all_gather(tokens, "tensor", axis=0, tiled=True)
    upstream = lax.all_gather(upstream_grad, "tensor", axis=0, tiled=True)
    mine = lax.all_to_all(
        upstream_grad.reshape(rows, n_dp, width // n_dp), "dp", split_axis=1, concat_axis=0
    )
    mine = lax.all_gather(mine.reshape(n_dp, rows, width // n_dp), "tensor", axis=1, tiled=True)
    mine = mine.reshape(-1, width // n_dp)
    gate_pre = jnp.dot(gathered, w_gate, preferred_element_type=jnp.float32)
    up_pre = jnp.dot(gathered, w_up, preferred_element_type=jnp.float32)
    sig_gate = jax.nn.sigmoid(gate_pre)
    act_gate = gate_pre * sig_gate
    hidden = (act_gate * up_pre).astype(jnp.bfloat16)
    hidden_all = lax.all_gather(hidden, "dp", axis=0, tiled=True)
    grad_hidden = contract_cols(upstream, w_down).astype(jnp.bfloat16)
    hidden_f = grad_hidden.astype(jnp.float32)
    grad_gate = (hidden_f * up_pre * sig_gate * (1.0 + gate_pre * (1.0 - sig_gate))).astype(
        jnp.bfloat16
    )
    grad_up = (hidden_f * act_gate).astype(jnp.bfloat16)
    factor = float(hidden_all.shape[0]) ** (-0.5)
    summed = lax.psum_scatter(
        (contract_cols(grad_gate, w_gate) + contract_cols(grad_up, w_up)).astype(jnp.bfloat16),
        "tensor",
        scatter_dimension=0,
        tiled=True,
    )
    grad_down = contract_rows(hidden_all, mine) * factor
    return (summed, grad_down)


MESH = pl.DeviceIdType.MESH
BF16 = jnp.bfloat16
F32 = jnp.float32
PARTS = 4
UNITS = 256


def kernel(
    n_dp, n_tensor,
    tok, upg, wg_h, wu_h, wd_h,
    gtok_h, gdown_h,
    wg, wu, wd, gt, gu, gate, up, gh, gboth, hid, upc, part, pc_out, pc_in, cs_out, cs_in,
    gtok, gdown,
    w_sem, loc_sem, out_sem,
    core_s, core_r, x_s, x_r, fwd_s, fwd_r,
    a2a_s, a2a_r, uc_s, uc_r, ux_s, ux_r, uf_s, uf_r,
    hy_s, hy_r, hz_s, hz_r, hf_s, hf_r,
    pc_s, pc_r, cs_s, cs_r,
):
    rows, width = tok.shape
    units = wg_h.shape[1]
    replica = rows * n_tensor
    step = width // PARTS
    mine = width // n_dp
    n_x, n_z = n_tensor // 2, n_dp // 2
    d, t = lax.axis_index("dp"), lax.axis_index("tensor")
    c, x = lax.rem(t, 2), lax.div(t, 2)
    y, z = lax.rem(d, 2), lax.div(d, 2)
    core = (d, x * 2 + 1 - c)
    ypeer = (z * 2 + 1 - y, t)
    xs, zs = range(1, n_x), range(1, n_z)
    pieces = [(f, min(UNITS, units - f)) for f in range(0, units, UNITS)]

    def x_to(o):
        return (d, lax.rem(x + o, n_x) * 2 + c)

    def x_from(o):
        return lax.rem(x + n_x - o, n_x) * 2 + c

    def z_from(o):
        partner = (z + 1 - 2 * lax.rem(z, 2), lax.rem(z + 2, 4), 3 - z)[o - 1]
        return partner * 2 + y

    def z_to(o):
        return (z_from(o), t)

    def dp_to(o):
        return lax.rem(d + o, n_dp)

    def of_tensor(i):
        return pl.ds(pl.multiple_of(i * rows, rows), rows)

    def of_chip(o):
        return pl.ds(pl.multiple_of(lax.rem(x + n_x - o, n_x) * 2 * rows, 2 * rows), 2 * rows)

    def cut(k):
        return pl.ds(k * step, step)

    def remote(src, dst, s, r, to):
        return pltpu.make_async_remote_copy(
            src_ref=src, dst_ref=dst, send_sem=s, recv_sem=r, device_id=to, device_id_type=MESH
        )

    loads = [[
        pltpu.make_async_copy(wg_h.at[cut(k), :], wg.at[cut(k), :], w_sem.at[0, k]),
        pltpu.make_async_copy(wu_h.at[cut(k), :], wu.at[cut(k), :], w_sem.at[1, k]),
        pltpu.make_async_copy(wd_h.at[:, cut(k)], wd.at[:, cut(k)], w_sem.at[2, k]),
    ] for k in range(PARTS)]
    own = [
        pltpu.make_async_copy(tok, gt.at[of_tensor(t), :], loc_sem.at[0]),
        pltpu.make_async_copy(upg, gu.at[of_tensor(t), :], loc_sem.at[1]),
        pltpu.make_async_copy(
            upg.at[:, pl.ds(pl.multiple_of(d * mine, mine), mine)],
            upc.at[d, of_tensor(t), :], loc_sem.at[2]),
    ]
    for copy in own:
        copy.start()
    for k in range(2):
        loads[k][0].start()
        loads[k][1].start()

    barrier = pltpu.get_barrier_semaphore()
    pl.semaphore_signal(barrier, inc=1, device_id=core, device_id_type=MESH)
    for o in xs:
        pl.semaphore_signal(barrier, inc=1, device_id=x_to(o), device_id_type=MESH)
    for o in range(1, n_dp):
        pl.semaphore_signal(barrier, inc=1, device_id=(dp_to(o), t), device_id_type=MESH)
    pl.semaphore_wait(barrier, 1 + (n_x - 1) + (n_dp - 1))
    own[0].wait()
    own[1].wait()

    to_core, to_x, passed = {}, {}, {}
    for a, all_rows in enumerate((gt, gu)):
        for k in range(PARTS):
            here = all_rows.at[of_tensor(t), cut(k)]
            to_core[a, k] = remote(
                here, here,
                core_s.at[a, k], core_r.at[a, k], core)
            for o in xs:
                to_x[a, k, o] = remote(
                    here, here,
                    x_s.at[a, k, o - 1], x_r.at[a, k, o - 1], x_to(o))
                there = all_rows.at[of_tensor(x_from(o)), cut(k)]
                passed[a, k, o] = remote(
                    there, there, fwd_s.at[a, k, o - 1], fwd_r.at[a, k, o - 1], core)
    for k in range(PARTS):
        for o in xs:
            to_x[0, k, o].start()
        to_core[0, k].start()
    exchange = [
        remote(
            gu.at[of_tensor(t), pl.ds(pl.multiple_of(dp_to(o) * mine, mine), mine)],
            upc.at[d, of_tensor(t), :],
            a2a_s.at[o - 1], a2a_r.at[o - 1], (dp_to(o), t))
        for o in range(1, n_dp)
    ]
    for copy in exchange:
        copy.start()
    for k in range(PARTS):
        to_core[1, k].start()

    def arrive(a, k):
        for o in xs:
            to_x[a, k, o].wait_recv()
            passed[a, k, o].start()

    def complete(a, k):
        to_core[a, k].wait_recv()
        for o in xs:
            passed[a, k, o].wait_recv()

    hid_y, hid_z, hid_f = {}, {}, {}
    for s in range(n_x):
        for j in range(len(pieces)):
            here = hid[j].at[d, of_chip(s), :]
            hid_y[s, j] = remote(here, here, hy_s.at[s, j], hy_r.at[s, j], ypeer)
            for o in zs:
                hid_z[s, j, o] = remote(
                    here, here, hz_s.at[s, j, o - 1], hz_r.at[s, j, o - 1], z_to(o))
                there = hid[j].at[z_from(o), of_chip(s), :]
                hid_f[s, j, o] = remote(
                    there, there, hf_s.at[s, j, o - 1], hf_r.at[s, j, o - 1], ypeer)

    def pass_hidden(s, j):
        for o in zs:
            hid_z[s, j, o].wait_recv()
            hid_f[s, j, o].start()

    def forward(s, k):
        lhs = gt[of_chip(s), k * step:(k + 1) * step]
        for j, (f, n) in enumerate(pieces):
            fs, ks = slice(f, f + n), slice(k * step, (k + 1) * step)
            g = jnp.dot(lhs, wg[ks, fs], preferred_element_type=F32)
            u = jnp.dot(lhs, wu[ks, fs], preferred_element_type=F32)
            if k > 0:
                g, u = gate[of_chip(s), fs] + g, up[of_chip(s), fs] + u
            gate[of_chip(s), fs] = g
            up[of_chip(s), fs] = u
            if k == PARTS - 1:
                hid[j][d, of_chip(s), :] = (g * jax.nn.sigmoid(g) * u).astype(BF16)
                for o in zs:
                    hid_z[s, j, o].start()
                hid_y[s, j].start()

    for k in range(PARTS):
        to_core[0, k].wait_recv()
        loads[k][0].wait()
        loads[k][1].wait()
        if k + 2 < PARTS:
            loads[k + 2][0].start()
            loads[k + 2][1].start()
        forward(0, k)
    for k in range(PARTS):
        arrive(0, k)
        for o in xs:
            to_x[1, k, o].start()
        loads[k][2].start()
        for o in xs:
            passed[0, k, o].wait_recv()
            forward(o, k)

    own[2].wait()
    for copy in exchange:
        copy.wait_recv()
    block = upc.at[:, of_tensor(t), :]
    up_core = remote(block, block, uc_s, uc_r, core)
    up_core.start()
    up_x, up_f = {}, {}
    for o in xs:
        up_x[o] = remote(block, block, ux_s.at[o - 1], ux_r.at[o - 1], x_to(o))
        there = upc.at[:, of_tensor(x_from(o)), :]
        up_f[o] = remote(there, there, uf_s.at[o - 1], uf_r.at[o - 1], core)

    for k in range(PARTS):
        arrive(1, k)
        complete(1, k)
        loads[k][2].wait()
        ks = slice(k * step, (k + 1) * step)
        lhs = gu[:, ks]
        for f, n in pieces:
            fs = slice(f, f + n)
            p = contract_cols(wd[fs, ks], lhs)
            if k > 0:
                p = gh[fs, :] + p
            gh[fs, :] = p
        pass_hidden(0, k)
    for o in xs:
        up_x[o].start()
    for f, n in pieces:
        fs = slice(f, f + n)
        g, u = gate[:, fs], up[:, fs]
        h = gh[fs, :].T.astype(BF16).astype(F32)
        sig = jax.nn.sigmoid(g)
        gboth[:, fs] = (h * u * sig * (1.0 + g * (1.0 - sig))).astype(BF16)
        gboth[:, units + f:units + f + n] = (h * (g * sig)).astype(BF16)

    swap, chip = {}, {}
    for q in range(PARTS):
        swap[q] = remote(
            pc_out.at[:, :, cut(q)], pc_in.at[:, :, cut(q)], pc_s.at[q], pc_r.at[q], core)
        for o in xs:
            chip[q, o] = remote(
                cs_out.at[o - 1, :, cut(q)], cs_in.at[o - 1, :, cut(q)],
                cs_s.at[q, o - 1], cs_r.at[q, o - 1], x_to(o))

    def add_cores(q):
        swap[q].wait_recv()
        qs = slice(q * step, (q + 1) * step)
        for o in xs:
            to = lax.rem(x + o, n_x)
            both = part[of_tensor(to * 2 + c), qs] + pc_in[to, :, qs].astype(F32)
            cs_out[o - 1, :, qs] = both.astype(BF16)
            chip[q, o].start()

    for q in range(PARTS):
        qs = slice(q * step, (q + 1) * step)
        both = contract_cols(wg[qs, :], gboth[:, :units]) + contract_cols(
            wu[qs, :], gboth[:, units:])
        part[:, qs] = both.T
        for i in range(n_x):
            pc_out[i, :, qs] = part[of_tensor(i * 2 + 1 - c), qs].astype(BF16)
        swap[q].start()
        if q > 0:
            add_cores(q - 1)
        if q == 2:
            pass_hidden(1, 0)
    add_cores(PARTS - 1)
    pass_hidden(1, 1)
    for o in xs:
        up_x[o].wait_recv()
        up_f[o].start()
    pass_hidden(1, 2)
    for q in range(PARTS):
        qs = slice(q * step, (q + 1) * step)
        total = part[of_tensor(t), qs] + pc_in[x, :, qs].astype(F32)
        for o in xs:
            chip[q, o].wait_recv()
            total = total + cs_in[o - 1, :, qs].astype(F32)
        gtok[:, qs] = total.astype(BF16)
    results = [pltpu.make_async_copy(gtok, gtok_h, out_sem.at[len(pieces)])]
    results[0].start()

    up_core.wait_recv()
    for o in xs:
        up_f[o].wait_recv()
    factor = float(n_dp * replica) ** (-0.5)
    pass_hidden(1, 3)
    for j, (f, n) in enumerate(pieces):
        for s in range(n_x):
            hid_y[s, j].wait_recv()
            for o in zs:
                hid_f[s, j, o].wait_recv()
        fs = slice(f, f + n)
        gdown[fs, :] = contract_rows(
            hid[j][...].reshape(n_dp * replica, n), upc[...].reshape(n_dp * replica, mine)
        ) * factor
        copy = pltpu.make_async_copy(
            gdown.at[pl.ds(f, n), :], gdown_h.at[pl.ds(f, n), :], out_sem.at[j])
        copy.start()
        results.append(copy)

    sent = [*to_core.values(), *to_x.values(), *passed.values(), *exchange, up_core,
            *up_x.values(), *up_f.values(), *hid_y.values(), *hid_z.values(), *hid_f.values(),
            *swap.values(), *chip.values()]
    for copy in sent:
        copy.wait_send()
    for copy in results:
        copy.wait()


PLACED = 4


def place(tokens_in, down_in, tokens_out, down_out, tokens_held, down_held, read, written):
    n = down_in.shape[0] // PLACED
    moves = [(tokens_in, tokens_held, tokens_out)]
    for i in range(PLACED):
        at = pl.ds(i * n, n)
        moves.append((down_in.at[at, :], down_held.at[at, :], down_out.at[at, :]))
    ins = [pltpu.make_async_copy(a, b, read.at[i]) for i, (a, b, _) in enumerate(moves)]
    outs = [pltpu.make_async_copy(b, c, written.at[i]) for i, (_, b, c) in enumerate(moves)]
    for copy in ins:
        copy.start()
    for copy, then in zip(ins, outs):
        copy.wait()
        then.start()
    for copy in outs:
        copy.wait()


def body(tokens, upstream_grad, w_gate, w_up, w_down):
    n_dp, n_tensor = lax.axis_size("dp"), lax.axis_size("tensor")
    rows, width = tokens.shape
    units = w_gate.shape[1]
    mine = width // n_dp
    n_x, n_z = n_tensor // 2, n_dp // 2
    if rows % 16 or n_tensor % 2 or n_dp % 2 or n_x != 2 or n_z != 4 or len(range(0, units, UNITS)) != PARTS:
        return plain_body(tokens, upstream_grad, w_gate, w_up, w_down)
    replica = rows * n_tensor
    n_pieces = -(-units // UNITS)
    dma = pltpu.SemaphoreType.DMA
    vmem = pltpu.VMEM

    def pair(*shape):
        return [dma(shape), dma(shape)] if shape else [dma, dma]

    scratch = [
        vmem((width, units), BF16), vmem((width, units), BF16), vmem((units, width), BF16),
        vmem((replica, width), BF16), vmem((replica, width), BF16),
        vmem((replica, units), F32), vmem((replica, units), F32), vmem((units, replica), F32),
        vmem((replica, 2 * units), BF16),
        [vmem((n_dp, replica, min(UNITS, units - f)), BF16) for f in range(0, units, UNITS)],
        vmem((n_dp, replica, mine), BF16),
        vmem((replica, width), F32),
        vmem((n_x, rows, width), BF16), vmem((n_x, rows, width), BF16),
        vmem((n_x - 1, rows, width), BF16), vmem((n_x - 1, rows, width), BF16),
        vmem((rows, width), BF16), vmem((units, mine), F32),
        dma((3, PARTS)), dma((3,)), dma((n_pieces + 1,)),
        *pair(2, PARTS), *pair(2, PARTS, n_x - 1), *pair(2, PARTS, n_x - 1),
        *pair(n_dp - 1), *pair(), *pair(n_x - 1), *pair(n_x - 1),
        *pair(n_x, n_pieces), *pair(n_x, n_pieces, n_z - 1), *pair(n_x, n_pieces, n_z - 1),
        *pair(PARTS), *pair(PARTS, n_x - 1),
    ]
    grads = pl.pallas_call(
        functools.partial(kernel, n_dp, n_tensor),
        out_shape=(
            jax.ShapeDtypeStruct((rows, width), BF16),
            jax.ShapeDtypeStruct((units, mine), F32),
        ),
        in_specs=[pl.BlockSpec(memory_space=pl.ANY)] * 5,
        out_specs=(pl.BlockSpec(memory_space=pl.ANY),) * 2,
        scratch_shapes=scratch,
        compiler_params=pltpu.CompilerParams(
            collective_id=0, has_side_effects=True, vmem_limit_bytes=56 * 1024 * 1024
        ),
        cost_estimate=pl.CostEstimate(
            flops=2 * replica * width * units * 6, bytes_accessed=6 * width * units,
            transcendentals=replica * units,
        ),
    )(tokens, upstream_grad, w_gate, w_up, w_down)
    return pl.pallas_call(
        place,
        out_shape=tuple(jax.ShapeDtypeStruct(g.shape, g.dtype) for g in grads),
        in_specs=[pl.BlockSpec(memory_space=pltpu.HBM)] * 2,
        out_specs=(pl.BlockSpec(memory_space=pltpu.HBM),) * 2,
        scratch_shapes=[
            vmem((rows, width), BF16), vmem((units, mine), F32),
            dma((PLACED + 1,)), dma((PLACED + 1,)),
        ],
    )(*grads)


def solution(mesh):
    in_specs = (
        P(("dp", "tensor"), None),
        P(("dp", "tensor"), None),
        P(None, "tensor"),
        P(None, "tensor"),
        P("tensor", None),
    )
    out_specs = (P(("dp", "tensor"), None), P("tensor", "dp"))
    return jax.shard_map(body, mesh=mesh, in_specs=in_specs, out_specs=out_specs, check_vma=False)
```

```python
import functools

import jax
import jax.numpy as jnp
from jax import lax
from jax.experimental import pallas as pl
from jax.experimental.pallas import tpu as pltpu
from jax.sharding import PartitionSpec as P


def contract_rows(left, right):
    return lax.dot_general(
        left, right, (((0,), (0,)), ((), ())), preferred_element_type=jnp.float32
    )


def contract_cols(left, right):
    return lax.dot_general(
        left, right, (((1,), (1,)), ((), ())), preferred_element_type=jnp.float32
    )


def plain_body(tokens, upstream_grad, w_gate, w_up, w_down):
    n_dp = lax.axis_size("dp")
    rows, width = upstream_grad.shape
    gathered = lax.all_gather(tokens, "tensor", axis=0, tiled=True)
    upstream = lax.all_gather(upstream_grad, "tensor", axis=0, tiled=True)
    mine = lax.all_to_all(
        upstream_grad.reshape(rows, n_dp, width // n_dp), "dp", split_axis=1, concat_axis=0
    )
    mine = lax.all_gather(mine.reshape(n_dp, rows, width // n_dp), "tensor", axis=1, tiled=True)
    mine = mine.reshape(-1, width // n_dp)
    gate_pre = jnp.dot(gathered, w_gate, preferred_element_type=jnp.float32)
    up_pre = jnp.dot(gathered, w_up, preferred_element_type=jnp.float32)
    sig_gate = jax.nn.sigmoid(gate_pre)
    act_gate = gate_pre * sig_gate
    hidden = (act_gate * up_pre).astype(jnp.bfloat16)
    hidden_all = lax.all_gather(hidden, "dp", axis=0, tiled=True)
    grad_hidden = contract_cols(upstream, w_down).astype(jnp.bfloat16)
    hidden_f = grad_hidden.astype(jnp.float32)
    grad_gate = (hidden_f * up_pre * sig_gate * (1.0 + gate_pre * (1.0 - sig_gate))).astype(
        jnp.bfloat16
    )
    grad_up = (hidden_f * act_gate).astype(jnp.bfloat16)
    factor = float(hidden_all.shape[0]) ** (-0.5)
    summed = lax.psum_scatter(
        (contract_cols(grad_gate, w_gate) + contract_cols(grad_up, w_up)).astype(jnp.bfloat16),
        "tensor",
        scatter_dimension=0,
        tiled=True,
    )
    grad_down = contract_rows(hidden_all, mine) * factor
    return (summed, grad_down)


MESH = pl.DeviceIdType.MESH
BF16 = jnp.bfloat16
F32 = jnp.float32
PARTS = 4
UNITS = 256


def kernel(
    n_dp, n_tensor,
    tok, upg, wg_h, wu_h, wd_h,
    gtok_h, gdown_h,
    wg, wu, wd, gt, gu, gate, up, gh, gboth, hid, upc, part, pc_out, pc_in, cs_out, cs_in,
    gtok, gdown,
    w_sem, loc_sem, out_sem,
    core_s, core_r, x_s, x_r, fwd_s, fwd_r,
    a2a_s, a2a_r, uc_s, uc_r, ux_s, ux_r, uf_s, uf_r,
    hy_s, hy_r, hz_s, hz_r, hf_s, hf_r,
    pc_s, pc_r, cs_s, cs_r,
):
    rows, width = tok.shape
    units = wg_h.shape[1]
    replica = rows * n_tensor
    step = width // PARTS
    mine = width // n_dp
    n_x, n_z = n_tensor // 2, n_dp // 2
    d, t = lax.axis_index("dp"), lax.axis_index("tensor")
    c, x = lax.rem(t, 2), lax.div(t, 2)
    y, z = lax.rem(d, 2), lax.div(d, 2)
    core = (d, x * 2 + 1 - c)
    ypeer = (z * 2 + 1 - y, t)
    xs, zs = range(1, n_x), range(1, n_z)
    pieces = [(f, min(UNITS, units - f)) for f in range(0, units, UNITS)]

    def x_to(o):
        return (d, lax.rem(x + o, n_x) * 2 + c)

    def x_from(o):
        return lax.rem(x + n_x - o, n_x) * 2 + c

    def z_from(o):
        partner = (z + 1 - 2 * lax.rem(z, 2), lax.rem(z + 2, 4), 3 - z)[o - 1]
        return partner * 2 + y

    def z_mirror(o):
        return z_from(o) + 1 - 2 * y

    def z_to(o):
        return (z_from(o), t)

    def dp_to(o):
        return lax.rem(d + o, n_dp)

    def of_tensor(i):
        return pl.ds(pl.multiple_of(i * rows, rows), rows)

    def of_chip(o):
        return pl.ds(pl.multiple_of(lax.rem(x + n_x - o, n_x) * 2 * rows, 2 * rows), 2 * rows)

    def cut(k):
        return pl.ds(k * step, step)

    def remote(src, dst, s, r, to):
        return pltpu.make_async_remote_copy(
            src_ref=src, dst_ref=dst, send_sem=s, recv_sem=r, device_id=to, device_id_type=MESH
        )

    loads = [[
        pltpu.make_async_copy(wg_h.at[cut(k), :], wg.at[cut(k), :], w_sem.at[0, k]),
        pltpu.make_async_copy(wu_h.at[cut(k), :], wu.at[cut(k), :], w_sem.at[1, k]),
        pltpu.make_async_copy(wd_h.at[:, cut(k)], wd.at[:, cut(k)], w_sem.at[2, k]),
    ] for k in range(PARTS)]
    own = [
        pltpu.make_async_copy(tok, gt.at[of_tensor(t), :], loc_sem.at[0]),
        pltpu.make_async_copy(upg, gu.at[of_tensor(t), :], loc_sem.at[1]),
        pltpu.make_async_copy(
            upg.at[:, pl.ds(pl.multiple_of(d * mine, mine), mine)],
            upc.at[d, of_tensor(t), :], loc_sem.at[2]),
    ]
    for copy in own:
        copy.start()
    for k in range(2):
        loads[k][0].start()
        loads[k][1].start()

    barrier = pltpu.get_barrier_semaphore()
    pl.semaphore_signal(barrier, inc=1, device_id=core, device_id_type=MESH)
    for o in xs:
        pl.semaphore_signal(barrier, inc=1, device_id=x_to(o), device_id_type=MESH)
    for o in range(1, n_dp):
        pl.semaphore_signal(barrier, inc=1, device_id=(dp_to(o), t), device_id_type=MESH)
    pl.semaphore_wait(barrier, 1 + (n_x - 1) + (n_dp - 1))
    own[0].wait()
    own[1].wait()

    to_core, to_x, passed = {}, {}, {}
    for a, all_rows in enumerate((gt, gu)):
        for k in range(PARTS):
            here = all_rows.at[of_tensor(t), cut(k)]
            to_core[a, k] = remote(
                here, here,
                core_s.at[a, k], core_r.at[a, k], core)
            for o in xs:
                to_x[a, k, o] = remote(
                    here, here,
                    x_s.at[a, k, o - 1], x_r.at[a, k, o - 1], x_to(o))
                there = all_rows.at[of_tensor(x_from(o)), cut(k)]
                passed[a, k, o] = remote(
                    there, there, fwd_s.at[a, k, o - 1], fwd_r.at[a, k, o - 1], core)
    for k in range(PARTS):
        for o in xs:
            to_x[0, k, o].start()
        to_core[0, k].start()
    exchange = [
        remote(
            gu.at[of_tensor(t), pl.ds(pl.multiple_of(dp_to(o) * mine, mine), mine)],
            upc.at[d, of_tensor(t), :],
            a2a_s.at[o - 1], a2a_r.at[o - 1], (dp_to(o), t))
        for o in range(1, n_dp)
    ]
    for copy in exchange:
        copy.start()
    for k in range(PARTS):
        to_core[1, k].start()

    def arrive(a, k):
        for o in xs:
            to_x[a, k, o].wait_recv()
            passed[a, k, o].start()

    def complete(a, k):
        to_core[a, k].wait_recv()
        for o in xs:
            passed[a, k, o].wait_recv()

    hid_y, hid_z, hid_f = {}, {}, {}
    last = (n_x - 1, len(pieces) - 1)
    for s in range(n_x):
        for j in range(len(pieces)):
            here = hid[j].at[d, of_chip(s), :]
            hid_y[s, j] = remote(here, here, hy_s.at[s, j], hy_r.at[s, j], ypeer)
            for o in zs:
                hid_z[s, j, o] = remote(
                    here, here, hz_s.at[s, j, o - 1], hz_r.at[s, j, o - 1], z_to(o))
                there, to = hid[j].at[z_from(o), of_chip(s), :], ypeer
                if (s, j) == last:
                    there, to = here, (z_mirror(o), t)
                hid_f[s, j, o] = remote(
                    there, there, hf_s.at[s, j, o - 1], hf_r.at[s, j, o - 1], to)

    def pass_hidden(s, j):
        for o in zs:
            hid_z[s, j, o].wait_recv()
            hid_f[s, j, o].start()

    def forward(s, k):
        lhs = gt[of_chip(s), k * step:(k + 1) * step]
        for j, (f, n) in enumerate(pieces):
            fs, ks = slice(f, f + n), slice(k * step, (k + 1) * step)
            g = jnp.dot(lhs, wg[ks, fs], preferred_element_type=F32)
            u = jnp.dot(lhs, wu[ks, fs], preferred_element_type=F32)
            if k > 0:
                g, u = gate[of_chip(s), fs] + g, up[of_chip(s), fs] + u
            gate[of_chip(s), fs] = g
            up[of_chip(s), fs] = u
            if k == PARTS - 1:
                hid[j][d, of_chip(s), :] = (g * jax.nn.sigmoid(g) * u).astype(BF16)
                for o in zs:
                    hid_z[s, j, o].start()
                    if (s, j) == last:
                        hid_f[s, j, o].start()
                hid_y[s, j].start()

    for k in range(PARTS):
        to_core[0, k].wait_recv()
        loads[k][0].wait()
        loads[k][1].wait()
        if k + 2 < PARTS:
            loads[k + 2][0].start()
            loads[k + 2][1].start()
        forward(0, k)
    for k in range(PARTS):
        arrive(0, k)
        for o in xs:
            to_x[1, k, o].start()
        loads[k][2].start()
        for o in xs:
            passed[0, k, o].wait_recv()
            forward(o, k)
    pass_hidden(0, 0)

    own[2].wait()
    for copy in exchange:
        copy.wait_recv()
    block = upc.at[:, of_tensor(t), :]
    up_core = remote(block, block, uc_s, uc_r, core)
    up_core.start()
    up_x, up_f = {}, {}
    for o in xs:
        up_x[o] = remote(block, block, ux_s.at[o - 1], ux_r.at[o - 1], x_to(o))
        there = upc.at[:, of_tensor(x_from(o)), :]
        up_f[o] = remote(there, there, uf_s.at[o - 1], uf_r.at[o - 1], core)

    for k in range(PARTS):
        arrive(1, k)
        complete(1, k)
        loads[k][2].wait()
        ks = slice(k * step, (k + 1) * step)
        lhs = gu[:, ks]
        for f, n in pieces:
            fs = slice(f, f + n)
            p = contract_cols(wd[fs, ks], lhs)
            if k > 0:
                p = gh[fs, :] + p
            gh[fs, :] = p
        if k + 1 < PARTS:
            pass_hidden(0, k + 1)
    for o in xs:
        up_x[o].start()
    for f, n in pieces:
        fs = slice(f, f + n)
        g, u = gate[:, fs], up[:, fs]
        h = gh[fs, :].T.astype(BF16).astype(F32)
        sig = jax.nn.sigmoid(g)
        gboth[:, fs] = (h * u * sig * (1.0 + g * (1.0 - sig))).astype(BF16)
        gboth[:, units + f:units + f + n] = (h * (g * sig)).astype(BF16)

    swap, chip = {}, {}
    for q in range(PARTS):
        swap[q] = remote(
            pc_out.at[:, :, cut(q)], pc_in.at[:, :, cut(q)], pc_s.at[q], pc_r.at[q], core)
        for o in xs:
            chip[q, o] = remote(
                cs_out.at[o - 1, :, cut(q)], cs_in.at[o - 1, :, cut(q)],
                cs_s.at[q, o - 1], cs_r.at[q, o - 1], x_to(o))

    def add_cores(q):
        swap[q].wait_recv()
        qs = slice(q * step, (q + 1) * step)
        for o in xs:
            to = lax.rem(x + o, n_x)
            both = part[of_tensor(to * 2 + c), qs] + pc_in[to, :, qs].astype(F32)
            cs_out[o - 1, :, qs] = both.astype(BF16)
            chip[q, o].start()

    for q in range(PARTS):
        qs = slice(q * step, (q + 1) * step)
        both = contract_cols(wg[qs, :], gboth[:, :units]) + contract_cols(
            wu[qs, :], gboth[:, units:])
        part[:, qs] = both.T
        for i in range(n_x):
            pc_out[i, :, qs] = part[of_tensor(i * 2 + 1 - c), qs].astype(BF16)
        swap[q].start()
        if q > 0:
            add_cores(q - 1)
        if q == 2:
            pass_hidden(1, 0)
    add_cores(PARTS - 1)
    pass_hidden(1, 1)
    for o in xs:
        up_x[o].wait_recv()
        up_f[o].start()
    pass_hidden(1, 2)
    for q in range(PARTS):
        qs = slice(q * step, (q + 1) * step)
        total = part[of_tensor(t), qs] + pc_in[x, :, qs].astype(F32)
        for o in xs:
            chip[q, o].wait_recv()
            total = total + cs_in[o - 1, :, qs].astype(F32)
        gtok[:, qs] = total.astype(BF16)
    results = [pltpu.make_async_copy(gtok, gtok_h, out_sem.at[len(pieces)])]
    results[0].start()

    up_core.wait_recv()
    for o in xs:
        up_f[o].wait_recv()
    factor = float(n_dp * replica) ** (-0.5)
    for j, (f, n) in enumerate(pieces):
        if j == last[1]:
            for o in zs:
                hid_z[last[0], j, o].wait_recv()
        for s in range(n_x):
            hid_y[s, j].wait_recv()
            for o in zs:
                hid_f[s, j, o].wait_recv()
        fs = slice(f, f + n)
        gdown[fs, :] = contract_rows(
            hid[j][...].reshape(n_dp * replica, n), upc[...].reshape(n_dp * replica, mine)
        ) * factor
        copy = pltpu.make_async_copy(
            gdown.at[pl.ds(f, n), :], gdown_h.at[pl.ds(f, n), :], out_sem.at[j])
        copy.start()
        results.append(copy)

    sent = [*to_core.values(), *to_x.values(), *passed.values(), *exchange, up_core,
            *up_x.values(), *up_f.values(), *hid_y.values(), *hid_z.values(), *hid_f.values(),
            *swap.values(), *chip.values()]
    for copy in sent:
        copy.wait_send()
    for copy in results:
        copy.wait()


PLACED = 4


def place(tokens_in, down_in, tokens_out, down_out, tokens_held, down_held, read, written):
    n = down_in.shape[0] // PLACED
    moves = [(tokens_in, tokens_held, tokens_out)]
    for i in range(PLACED):
        at = pl.ds(i * n, n)
        moves.append((down_in.at[at, :], down_held.at[at, :], down_out.at[at, :]))
    ins = [pltpu.make_async_copy(a, b, read.at[i]) for i, (a, b, _) in enumerate(moves)]
    outs = [pltpu.make_async_copy(b, c, written.at[i]) for i, (_, b, c) in enumerate(moves)]
    for copy in ins:
        copy.start()
    for copy, then in zip(ins, outs):
        copy.wait()
        then.start()
    for copy in outs:
        copy.wait()


def body(tokens, upstream_grad, w_gate, w_up, w_down):
    n_dp, n_tensor = lax.axis_size("dp"), lax.axis_size("tensor")
    rows, width = tokens.shape
    units = w_gate.shape[1]
    mine = width // n_dp
    n_x, n_z = n_tensor // 2, n_dp // 2
    if rows % 16 or n_tensor % 2 or n_dp % 2 or n_x != 2 or n_z != 4 or len(range(0, units, UNITS)) != PARTS:
        return plain_body(tokens, upstream_grad, w_gate, w_up, w_down)
    replica = rows * n_tensor
    n_pieces = -(-units // UNITS)
    dma = pltpu.SemaphoreType.DMA
    vmem = pltpu.VMEM

    def pair(*shape):
        return [dma(shape), dma(shape)] if shape else [dma, dma]

    scratch = [
        vmem((width, units), BF16), vmem((width, units), BF16), vmem((units, width), BF16),
        vmem((replica, width), BF16), vmem((replica, width), BF16),
        vmem((replica, units), F32), vmem((replica, units), F32), vmem((units, replica), F32),
        vmem((replica, 2 * units), BF16),
        [vmem((n_dp, replica, min(UNITS, units - f)), BF16) for f in range(0, units, UNITS)],
        vmem((n_dp, replica, mine), BF16),
        vmem((replica, width), F32),
        vmem((n_x, rows, width), BF16), vmem((n_x, rows, width), BF16),
        vmem((n_x - 1, rows, width), BF16), vmem((n_x - 1, rows, width), BF16),
        vmem((rows, width), BF16), vmem((units, mine), F32),
        dma((3, PARTS)), dma((3,)), dma((n_pieces + 1,)),
        *pair(2, PARTS), *pair(2, PARTS, n_x - 1), *pair(2, PARTS, n_x - 1),
        *pair(n_dp - 1), *pair(), *pair(n_x - 1), *pair(n_x - 1),
        *pair(n_x, n_pieces), *pair(n_x, n_pieces, n_z - 1), *pair(n_x, n_pieces, n_z - 1),
        *pair(PARTS), *pair(PARTS, n_x - 1),
    ]
    grads = pl.pallas_call(
        functools.partial(kernel, n_dp, n_tensor),
        out_shape=(
            jax.ShapeDtypeStruct((rows, width), BF16),
            jax.ShapeDtypeStruct((units, mine), F32),
        ),
        in_specs=[pl.BlockSpec(memory_space=pl.ANY)] * 5,
        out_specs=(pl.BlockSpec(memory_space=pl.ANY),) * 2,
        scratch_shapes=scratch,
        compiler_params=pltpu.CompilerParams(
            collective_id=0, has_side_effects=True, vmem_limit_bytes=56 * 1024 * 1024
        ),
        cost_estimate=pl.CostEstimate(
            flops=2 * replica * width * units * 6, bytes_accessed=6 * width * units,
            transcendentals=replica * units,
        ),
    )(tokens, upstream_grad, w_gate, w_up, w_down)
    return pl.pallas_call(
        place,
        out_shape=tuple(jax.ShapeDtypeStruct(g.shape, g.dtype) for g in grads),
        in_specs=[pl.BlockSpec(memory_space=pltpu.HBM)] * 2,
        out_specs=(pl.BlockSpec(memory_space=pltpu.HBM),) * 2,
        scratch_shapes=[
            vmem((rows, width), BF16), vmem((units, mine), F32),
            dma((PLACED + 1,)), dma((PLACED + 1,)),
        ],
    )(*grads)


def solution(mesh):
    in_specs = (
        P(("dp", "tensor"), None),
        P(("dp", "tensor"), None),
        P(None, "tensor"),
        P(None, "tensor"),
        P("tensor", None),
    )
    out_specs = (P(("dp", "tensor"), None), P("tensor", "dp"))
    return jax.shard_map(body, mesh=mesh, in_specs=in_specs, out_specs=out_specs, check_vma=False)
```
